32 devices in a mesh: layer: 2 (over x), example: 16 (over z, y, core).
Axes of the slice: x: 2, y: 2, z: 4, core: 2. Of those that a mesh axis runs over, the one named last changes fastest.
Arguments:
- adapter_input: bfloat16 [2, 8, 65536], P('layer', None, 'example'), may hold values from -4 to 4
- output_gradient: bfloat16 [2, 65536, 512], P('layer', 'example'), may hold values from -4 to 4
- projection: bfloat16 [2, 4, 512, 128], P('layer'), may hold values from -0.25 to 0.25
- input_block_index: int32 [2, 4, 4], P('layer'), may hold values from 0 to 31
- turn_token_length: int32 [2048], P('example'), may hold values from 1 to 32, as said below
- turn_to_example: int32 [2048], P('example'), may hold values from 0 to 1023, as said below
Outputs:
- factor: float32 [512, 512], P('example')
- whitened: float32 [1024, 512], P(('example', 'layer'))
The draws below stay inside these ranges and needn't reach their ends.
Inputs may be any that keep to these rules, and one draw needn't show every extreme that they name: `turn_token_length`: within each shard of 128 turns the lengths add up to at most 4096. `turn_to_example`: the turns of shard s carry the example numbers s * 64 to (s + 1) * 64 - 1, never falling, each at least once.
All inputs are finite; a program needn't handle non-finite values.
Results may differ from the reference program's by a relative error of at most 0.0033.
Values sent between devices are 32-bit elements; how exact they have to be, the bound alone decides.
A program may use at most 64 MiB of HBM per device.

```python
import math
import jax
import jax.numpy as jnp
from jax import lax

KV = 512
ADAPTER_RANK = 8
F = 512
NPICK = 4
MAXLEN = 32
EX_DEV = 64
TURNS_DEV = 128
SHARD_TOKENS = 4096
FBLK = 4
NBLK = 32
LAYER_COUNT = 2
TURNS = 2048
TOKEN_SLOTS = 65536
EXAMPLES = 1024


def draw_turn_token_length(key, part):
    shards = TURNS // TURNS_DEV
    key_caps, key_busy, key_raw, key_long = jax.random.split(jax.random.fold_in(key, 11), 4)
    caps = jax.random.randint(key_caps, (shards,), 1, MAXLEN + 1)
    busiest = jax.random.randint(key_busy, (), 0, shards)
    shard_ids = jnp.arange(shards)
    caps = jnp.where(shard_ids == busiest, MAXLEN, caps)
    raw_bits = jax.random.randint(key_raw, (shards, TURNS_DEV), 0, 1 << 20)
    lengths = 1 + raw_bits % caps[:, None]
    longest = jax.random.randint(key_long, (), 0, TURNS_DEV)
    chosen = (shard_ids[:, None] == busiest) & (jnp.arange(TURNS_DEV)[None, :] == longest)
    lengths = jnp.where(chosen, MAXLEN, lengths)
    return lengths.reshape(-1).astype(jnp.int32)


def draw_turn_to_example(key, part):
    shards = TURNS // TURNS_DEV
    shard_keys = jax.random.split(jax.random.fold_in(key, 23), shards)

    def one_shard(shard_key):
        order = jax.random.permutation(shard_key, TURNS_DEV - 1)
        cuts = (order < EX_DEV - 1).astype(jnp.int32)
        return jnp.concatenate([jnp.zeros((1,), jnp.int32), jnp.cumsum(cuts).astype(jnp.int32)])
    local_ids = jax.vmap(one_shard)(shard_keys)
    offsets = EX_DEV * jnp.arange(shards, dtype=jnp.int32)
    return (local_ids + offsets[:, None]).reshape(-1).astype(jnp.int32)


def touch_ends(values, stream_key, low, largest):
    shape = values.shape
    index_at = [jax.random.randint(jax.random.fold_in(stream_key, axis), (), 0, shape[axis]) for axis in range(len(shape))]
    values = values.at[tuple(index_at)].set(low)
    longest = shape.index(max(shape))
    index_at[longest] = (index_at[longest] + 1) % shape[longest]
    return values.at[tuple(index_at)].set(largest)


def block_scale(key, dims, cuts, smallest, largest):
    def one(dim, parts):
        heights = jax.random.uniform(jax.random.fold_in(jax.random.fold_in(key, 6), dim), (parts,), jnp.float32, smallest / len(cuts), largest / len(cuts))
        return jnp.repeat(jnp.exp(heights), dims[dim] // parts).reshape((-1,) + (1,) * (len(dims) - dim - 1))

    loudness = one(*cuts[0])
    for cut in cuts[1:]:
        loudness = loudness * one(*cut)
    return loudness


def bell_draw(own_key, dims, width, limit, cuts=(), held_as=jnp.bfloat16):
    loudness = block_scale(own_key, dims, cuts, -0.22, 0.18) if cuts else 1.0
    drawn = jax.random.normal(own_key, dims, jnp.float32) * width * loudness
    return jnp.minimum(jnp.maximum(drawn, -limit), limit).astype(held_as)


def setup_inputs(seed: int = 0) -> dict:
    key_list = jax.random.split(jax.random.key(seed), 7)
    adapter_input = bell_draw(key_list[0], (LAYER_COUNT, ADAPTER_RANK, TOKEN_SLOTS), 0.5, 4.0, ((0, 2), (2, 16)))
    output_gradient = bell_draw(key_list[1], (LAYER_COUNT, TOKEN_SLOTS, KV), 0.5, 4.0, ((0, 2), (1, 16)))
    projection = bell_draw(key_list[2], (LAYER_COUNT, FBLK, NPICK * 128, 128), (NPICK * 128) ** -0.5, 0.25, ((0, 2),))
    input_block_index = touch_ends(jax.random.randint(key_list[3], (LAYER_COUNT, FBLK, NPICK), 0, NBLK), jax.random.fold_in(key_list[3], 1), 0, NBLK - 1).astype(jnp.int32)
    turn_token_length = draw_turn_token_length(jax.random.fold_in(key_list[6], 71), 0)
    turn_to_example = draw_turn_to_example(jax.random.fold_in(key_list[6], 71), 0)
    return dict(adapter_input=adapter_input, output_gradient=output_gradient, projection=projection, input_block_index=input_block_index, turn_token_length=turn_token_length, turn_to_example=turn_to_example)


def slot_owners(turn_token_length, turn_to_example):
    shards = TURNS // TURNS_DEV
    lengths = turn_token_length.reshape(shards, TURNS_DEV).astype(jnp.int32)
    offsets = (EX_DEV * jnp.arange(shards, dtype=jnp.int32))[:, None]
    owners = turn_to_example.reshape(shards, TURNS_DEV).astype(jnp.int32) - offsets
    turn_ends = jnp.cumsum(lengths, axis=1).astype(jnp.int32)
    starts = turn_ends - lengths
    position = jnp.arange(SHARD_TOKENS, dtype=jnp.int32)
    inside = (position[None, None, :] >= starts[:, :, None]) & (position[None, None, :] < turn_ends[:, :, None])
    marked = lax.optimization_barrier(jnp.sum(jnp.where(inside, owners[:, :, None] + 1, 0), axis=1)).astype(jnp.int32) - 1
    return jnp.where(marked < 0, EX_DEV, marked).astype(jnp.int32)

def reference(adapter_input, output_gradient, projection, input_block_index, turn_token_length, turn_to_example):
    shards = TURNS // TURNS_DEV
    owner_all = slot_owners(turn_token_length, turn_to_example)

    def shard_features(shard):
        first_token = shard * SHARD_TOKENS
        owner = lax.dynamic_index_in_dim(owner_all, shard, 0, keepdims=False)
        running = jnp.zeros((EX_DEV, F), jnp.float32)
        for layer_number in range(LAYER_COUNT):
            activation_block = lax.dynamic_slice_in_dim(adapter_input[layer_number], first_token, SHARD_TOKENS, 1).astype(jnp.float32)
            grad_block = lax.dynamic_slice_in_dim(output_gradient[layer_number], first_token, SHARD_TOKENS, 0).astype(jnp.float32)
            outer = (activation_block.T[:, :, None] * grad_block[:, None, :]).reshape(SHARD_TOKENS, ADAPTER_RANK * KV)
            gradient_value = jax.ops.segment_sum(outer, owner, num_segments=EX_DEV + 1)[:EX_DEV].astype(jnp.bfloat16)
            blocks = gradient_value.reshape(EX_DEV, NBLK, 128)
            pieces = []
            for column in range(FBLK):
                chosen = jnp.take(blocks, input_block_index[layer_number, column], axis=1).reshape(EX_DEV, NPICK * 128)
                pieces.append(jnp.dot(chosen.astype(jnp.float32), projection[layer_number, column].astype(jnp.float32), preferred_element_type=jnp.float32))
            running = running + jnp.concatenate(pieces, axis=1)
        return running
    features = lax.map(shard_features, jnp.arange(shards, dtype=jnp.int32)).reshape(EXAMPLES, F)
    gram = jnp.dot(features.T.astype(jnp.float32), features.astype(jnp.float32), precision=lax.Precision.HIGHEST, preferred_element_type=jnp.float32)
    lower_factor = jnp.linalg.cholesky(gram)
    scale = math.sqrt(EXAMPLES)
    factor = lower_factor.T / scale
    whitened = jax.scipy.linalg.solve_triangular(lower_factor, features.T, lower=True).T * scale
    return (factor, whitened)
```

```python
import functools
import math

import jax
import jax.numpy as jnp
from jax import lax
from jax.experimental import pallas as pl
from jax.experimental.pallas import tpu as pltpu
from jax.sharding import PartitionSpec as P

EX_DEV = 64
LANES = 128
F32 = jnp.float32
BF16 = jnp.bfloat16
MESH = pl.DeviceIdType.MESH


def mm(a, b):
    return jnp.dot(a, b, preferred_element_type=F32)


def mm_t(a, b):
    return lax.dot_general(a, b, (((1,), (1,)), ((), ())), preferred_element_type=F32)


def mm_tn(a, b):
    return lax.dot_general(a, b, (((0,), (0,)), ((), ())), preferred_element_type=F32)


def split(x):
    high = x.astype(BF16)
    return high, (x - high.astype(F32)).astype(BF16)


def three(dot, a, b):
    return dot(a[0], b[0]) + (dot(a[0], b[1]) + dot(a[1], b[0]))


def gram_kernel(
    layers, shards, pieces, chunk,
    idx_ref, lens_ref, own_ref, a_ref, g_hbm, proj_ref,
    gram_ref, feat_ref,
    g_buf, acc, grad, part, part_in, both, packed, rs_in,
    g_sem, px_send, px_recv, fx_send, fx_recv, rs_send, rs_recv,
    ag_send, ag_recv, xf_send, xf_recv, cf_send, cf_recv,
):
    layer = lax.axis_index("layer")
    shard = lax.axis_index("example")
    peers = shards // 2
    spot = shard // 2
    core = shard % 2
    mate = spot * 2 + (1 - core)

    def to_layer(d):
        return ((layer + d) % layers, shard)

    def to_spot(d):
        return (layer, ((spot + d) % peers) * 2 + core)

    loads = []
    rows = g_hbm.shape[0] // pieces
    for i in range(pieces):
        cut = pl.ds(i * rows, rows)
        load = pltpu.make_async_copy(g_hbm.at[cut], g_buf.at[cut], g_sem.at[i])
        load.start()
        loads.append(load)

    barrier = pltpu.get_barrier_semaphore()
    targets = [to_layer(d) for d in range(1, layers)]
    targets += [to_spot(d) for d in range(1, peers)] + [(layer, mate)]
    for target in targets:
        pl.semaphore_signal(barrier, inc=1, device_id=target, device_id_type=MESH)

    lens = lens_ref[...].astype(F32)
    local = own_ref[...] - shard * EX_DEV
    example = lax.broadcasted_iota(jnp.int32, (EX_DEV, lens.shape[1]), 0)
    start = jnp.sum(jnp.where(local < example, lens, 0.0), axis=1, keepdims=True)
    end = jnp.sum(jnp.where(local <= example, lens, 0.0), axis=1, keepdims=True)
    rank = a_ref.shape[0]
    for i in range(pieces):
        place = (lax.broadcasted_iota(jnp.int32, (EX_DEV, rows), 1) + i * rows).astype(F32)
        mask = jnp.where((place >= start) & (place < end), 1.0, 0.0).astype(BF16)
        weighted = jnp.concatenate(
            [mask * a_ref[r : r + 1, i * rows : (i + 1) * rows] for r in range(rank)], axis=0
        )
        loads[i].wait()
        product = mm(weighted, g_buf[i * rows : (i + 1) * rows, :])
        if i == 0:
            acc[...] = product
        else:
            acc[...] += product
    width = g_hbm.shape[1] // LANES
    for r in range(rank):
        for w in range(width):
            grad[r * width + w] = acc[
                r * EX_DEV : (r + 1) * EX_DEV, w * LANES : (w + 1) * LANES
            ].astype(BF16)
    blocks, depth = proj_ref.shape[0], proj_ref.shape[1] // LANES
    for j in range(blocks):
        chosen = jnp.concatenate([grad[idx_ref[j, k]] for k in range(depth)], axis=1)
        part[:, j * LANES : (j + 1) * LANES] = mm(chosen, proj_ref[j])

    pl.semaphore_wait(barrier, len(targets))
    sends = []

    def push(src, dst, send_sem, recv_sem, target):
        copy = pltpu.make_async_remote_copy(
            src_ref=src, dst_ref=dst, send_sem=send_sem, recv_sem=recv_sem,
            device_id=target, device_id_type=MESH,
        )
        copy.start()
        sends.append(copy)
        return copy

    copies = [
        push(part, part_in.at[d - 1], px_send.at[d - 1], px_recv.at[d - 1], to_layer(d))
        for d in range(1, layers)
    ]
    for copy in copies:
        copy.wait_recv()
    total = part[...]
    for d in range(1, layers):
        total = total + part_in[d - 1]
    both[0] = total

    copy = push(both.at[0], both.at[1], fx_send, fx_recv, (layer, mate))
    owned = EX_DEV // layers
    feat_ref[...] = both[0, pl.ds(pl.multiple_of(layer * owned, 8), owned), :]
    copy.wait_recv()

    pair = jnp.concatenate([both[0], both[1]], axis=0)
    high, low = split(pair)
    row = 0
    for i in range(blocks):
        cut = slice(i * LANES, (i + 1) * LANES)
        strip = three(
            mm_tn, (high[:, cut], low[:, cut]), (high[:, i * LANES :], low[:, i * LANES :])
        )
        for j in range(blocks - i):
            packed[row : row + LANES, :] = strip[:, j * LANES : (j + 1) * LANES]
            row += LANES
    if row < packed.shape[0]:
        packed[row:, :] = jnp.zeros((packed.shape[0] - row, LANES), F32)

    def where(lay, cor, spo):
        return pl.multiple_of(((lay * 2 + cor) * peers + spo) * chunk, 8)

    mine = where(layer, core, spot)
    copies = []
    for d in range(1, peers):
        source = where(layer, core, (spot + d) % peers)
        copies.append(push(
            packed.at[pl.ds(source, chunk)], rs_in.at[d - 1],
            rs_send.at[d - 1], rs_recv.at[d - 1], to_spot(d),
        ))
    total = packed[pl.ds(mine, chunk), :]
    for d in range(1, peers):
        copies[d - 1].wait_recv()
        total = total + rs_in[d - 1]
    gram_ref[pl.ds(mine, chunk), :] = total

    gathers = []
    here = gram_ref.at[pl.ds(mine, chunk)]
    for d in range(1, peers):
        gathers.append(push(here, here, ag_send.at[d - 1], ag_recv.at[d - 1], to_spot(d)))
    forwards = []
    for d in range(peers):
        if d:
            gathers[d - 1].wait_recv()
        got = gram_ref.at[pl.ds(where(layer, core, (spot - d + peers) % peers), chunk)]
        for x in range(1, layers):
            forwards.append(push(got, got, xf_send.at[x - 1, d], xf_recv.at[x - 1, d], to_layer(x)))
    pairs = []
    for x in range(layers):
        if x:
            for d in range(peers):
                forwards[d * (layers - 1) + x - 1].wait_recv()
        got = gram_ref.at[pl.ds(where((layer - x + layers) % layers, core, 0), peers * chunk)]
        pairs.append(push(got, got, cf_send.at[x], cf_recv.at[x], (layer, mate)))
    for copy in pairs:
        copy.wait_recv()
    for copy in sends:
        copy.wait_send()


def diagonal(shape):
    return lax.broadcasted_iota(jnp.int32, shape, 0) == lax.broadcasted_iota(jnp.int32, shape, 1)


def factor_kernel(
    scale, blocks, gram_ref, feat_ref, band_ref, white_ref,
    full, b_high, b_low, x_ref, inv, work,
):
    size = blocks * LANES
    half = size // 2
    row = 0
    for i in range(blocks):
        for j in range(i, blocks):
            block = gram_ref[row : row + LANES, :]
            row += LANES
            full[i * LANES : (i + 1) * LANES, j * LANES : (j + 1) * LANES] = block
            if j > i:
                full[j * LANES : (j + 1) * LANES, i * LANES : (i + 1) * LANES] = block.T
    gram = full[...]
    eye = diagonal((size, size))
    kept = jnp.where(eye, gram, 0.0)
    inv_row = lax.rsqrt(jnp.sum(kept, axis=0, keepdims=True))
    inv_col = lax.rsqrt(jnp.sum(kept, axis=1, keepdims=True))
    inv[...] = inv_row
    scaled = gram * inv_col * inv_row
    full[...] = scaled
    high, low = split(scaled)
    b_high[...] = high
    b_low[...] = low
    bound = jnp.max(jnp.sum(jnp.abs(scaled), axis=0, keepdims=True))
    first = 2.5 / jnp.full((1, size), bound, F32)
    rows = lax.broadcasted_iota(jnp.int32, (size, size), 0)
    cols = lax.broadcasted_iota(jnp.int32, (size, size), 1)
    root = jnp.sqrt(first)
    x_ref[...] = jnp.where(
        rows > cols, -first * scaled * root,
        jnp.where(eye, root * (1.5 - 0.5 * first * scaled), 0.0),
    )

    corner = diagonal((half, half))
    lower = lax.broadcasted_iota(jnp.int32, (half, half), 0) > lax.broadcasted_iota(
        jnp.int32, (half, half), 1
    )
    ident = jnp.where(corner, 1.0, 0.0)

    def half_low(e):
        return jnp.where(lower, e, jnp.where(corner, 0.5 * e, 0.0))

    def step(fine):
        top = x_ref[:half, :half]
        bottom = x_ref[half:, :]
        bh = b_high[...]
        if fine:
            bl = b_low[...]
            top_s, bottom_s = split(top), split(bottom)
            y0 = three(mm, top_s, (bh[:half, :half], bl[:half, :half]))
            y1 = three(mm, bottom_s, (bh, bl))
            y0_s, y1_s = split(y0), split(y1)
            e0 = three(mm_t, y0_s, top_s) - ident
            e1 = three(mm_t, (y1_s[0][:, :half], y1_s[1][:, :half]), top_s)
            e2 = three(mm_t, y1_s, bottom_s) - ident
            top_h, bottom_h = top_s[0], bottom_s[0]
        else:
            top_h, bottom_h = top.astype(BF16), bottom.astype(BF16)
            y0 = mm(top_h, bh[:half, :half]).astype(BF16)
            y1 = mm(bottom_h, bh).astype(BF16)
            e0 = mm_t(y0, top_h) - ident
            e1 = mm_t(y1[:, :half], top_h)
            e2 = mm_t(y1, bottom_h) - ident
        p0 = half_low(e0).astype(BF16)
        p1 = e1.astype(BF16)
        p2 = half_low(e2).astype(BF16)
        x_ref[:half, :half] = top - mm(p0, top_h)
        x_ref[half:, :half] = bottom[:, :half] - (mm(p1, top_h) + mm(p2, bottom_h[:, :half]))
        x_ref[half:, half:] = bottom[:, half:] - mm(p2, bottom_h[:, half:])
        return e0, e1, e2

    def norm(errors):
        e0, e1, e2 = errors
        return jnp.sum(e0 * e0 + 2.0 * (e1 * e1) + e2 * e2)

    def body(fine, state):
        return state[0] + 1, norm(step(fine))

    def blind(_, carry):
        step(False)
        return carry

    lax.fori_loop(0, 6, blind, 0)
    state = lax.while_loop(
        lambda s: (s[0] < 24) & jnp.logical_not(s[1] < 1.0),
        functools.partial(body, False), (jnp.int32(0), F32(1e9)),
    )
    state = lax.while_loop(
        lambda s: (s[0] < 8) & jnp.logical_not(s[1] < 1e-4),
        functools.partial(body, True), (jnp.int32(0), F32(1e9)),
    )
    good = state[1] < 1e-4

    @pl.when(jnp.logical_not(good))
    def _():
        work[:, :size] = full[...]
        work[:, size:] = jnp.where(eye, 1.0, 0.0)
        line = lax.broadcasted_iota(jnp.int32, (1, 2 * size), 1)
        down = lax.broadcasted_iota(jnp.int32, (size, 1), 0)

        def column(j, carry):
            pivot_row = work[pl.ds(j, 1), :]
            pivot = jnp.sum(jnp.where(line == j, pivot_row, 0.0), axis=1, keepdims=True)
            pivot_row = pivot_row / jnp.sqrt(pivot)
            left = work[:, :size]
            entry = jnp.sum(jnp.where(cols == j, left, 0.0), axis=1, keepdims=True)
            entry = jnp.where(down > j, entry / jnp.sqrt(pivot), 0.0)
            work[...] = work[...] - entry * pivot_row
            work[pl.ds(j, 1), :] = pivot_row
            return carry

        lax.fori_loop(0, size, column, 0)
        x_ref[...] = jnp.where(rows >= cols, work[:, size:], 0.0)

    side = band_ref.shape[0]
    begin = pl.multiple_of(lax.axis_index("example") * side, 8)
    over = 1.0 / (inv[...] * scale)
    band_rows = lax.broadcasted_iota(jnp.int32, (side, size), 0) + begin
    upper = lax.broadcasted_iota(jnp.int32, (side, size), 1) >= band_rows

    @pl.when(good)
    def _():
        band = three(mm, split(x_ref[pl.ds(begin, side), :]), (b_high[...], b_low[...]))
        band_ref[...] = jnp.where(upper, band * over, 0.0)

    @pl.when(jnp.logical_not(good))
    def _():
        band_ref[...] = jnp.where(upper, work[pl.ds(begin, side), :size] * over, 0.0)

    white_ref[...] = scale * three(mm_t, split(feat_ref[...] * inv[...]), split(x_ref[...]))


def shards(
    adapter_input,
    output_gradient,
    projection,
    input_block_index,
    turn_token_length,
    turn_to_example,
):
    layers, count = lax.axis_size("layer"), lax.axis_size("example")
    rank, tokens = adapter_input.shape[1:]
    width = output_gradient.shape[2]
    blocks, depth, _ = projection.shape[1:]
    size = blocks * LANES
    peers = count // 2
    pieces = 4
    packed_rows = blocks * (blocks + 1) // 2 * LANES
    owners = 2 * layers * peers
    chunk = -(-packed_rows // (owners * 8)) * 8
    vmem = pl.BlockSpec(memory_space=pltpu.VMEM)
    dma = pltpu.SemaphoreType.DMA
    near, far = max(layers - 1, 1), max(peers - 1, 1)
    gram, features = pl.pallas_call(
        functools.partial(gram_kernel, layers, count, pieces, chunk),
        out_shape=(
            jax.ShapeDtypeStruct((owners * chunk, LANES), F32),
            jax.ShapeDtypeStruct((EX_DEV // layers, size), F32),
        ),
        in_specs=[
            pl.BlockSpec(memory_space=pltpu.SMEM), vmem, vmem, vmem,
            pl.BlockSpec(memory_space=pl.ANY), vmem,
        ],
        out_specs=(vmem, vmem),
        scratch_shapes=[
            pltpu.VMEM((tokens, width), BF16),
            pltpu.VMEM((rank * EX_DEV, width), F32),
            pltpu.VMEM((rank * width // LANES, EX_DEV, LANES), BF16),
            pltpu.VMEM((EX_DEV, size), F32),
            pltpu.VMEM((near, EX_DEV, size), F32),
            pltpu.VMEM((2, EX_DEV, size), F32),
            pltpu.VMEM((owners * chunk, LANES), F32),
            pltpu.VMEM((far, chunk, LANES), F32),
            dma((pieces,)),
            dma((near,)), dma((near,)), dma(()), dma(()),
            dma((far,)), dma((far,)), dma((far,)), dma((far,)),
            dma((near, peers)), dma((near, peers)), dma((layers,)), dma((layers,)),
        ],
        compiler_params=pltpu.CompilerParams(
            collective_id=0, has_side_effects=True, vmem_limit_bytes=40 * 1024 * 1024
        ),
    )(
        input_block_index[0],
        turn_token_length.reshape(1, -1),
        turn_to_example.reshape(1, -1),
        adapter_input[0],
        output_gradient[0],
        projection[0],
    )
    return pl.pallas_call(
        functools.partial(factor_kernel, math.sqrt(EX_DEV * count), blocks),
        out_shape=(
            jax.ShapeDtypeStruct((size // count, size), F32),
            jax.ShapeDtypeStruct((EX_DEV // layers, size), F32),
        ),
        in_specs=[vmem, vmem],
        out_specs=(vmem, vmem),
        scratch_shapes=[
            pltpu.VMEM((size, size), F32),
            pltpu.VMEM((size, size), BF16),
            pltpu.VMEM((size, size), BF16),
            pltpu.VMEM((size, size), F32),
            pltpu.VMEM((1, size), F32),
            pltpu.VMEM((size, 2 * size), F32),
        ],
        compiler_params=pltpu.CompilerParams(vmem_limit_bytes=40 * 1024 * 1024),
    )(gram, features)


def solution(mesh):
    in_specs = (
        P("layer", None, "example"),
        P("layer", "example", None),
        P("layer", None, None, None),
        P("layer", None, None),
        P("example"),
        P("example"),
    )
    out_specs = (P("example", None), P(("example", "layer"), None))
    return jax.shard_map(shards, mesh=mesh, in_specs=in_specs, out_specs=out_specs, check_vma=False)
```

```python
import functools
import math

import jax
import jax.numpy as jnp
from jax import lax
from jax.experimental import pallas as pl
from jax.experimental.pallas import tpu as pltpu
from jax.sharding import PartitionSpec as P

EX_DEV = 64
LANES = 128
F32 = jnp.float32
BF16 = jnp.bfloat16
MESH = pl.DeviceIdType.MESH


def mm(a, b):
    return jnp.dot(a, b, preferred_element_type=F32)


def mm_t(a, b):
    return lax.dot_general(a, b, (((1,), (1,)), ((), ())), preferred_element_type=F32)


def mm_tn(a, b):
    return lax.dot_general(a, b, (((0,), (0,)), ((), ())), preferred_element_type=F32)


def split(x):
    high = x.astype(BF16)
    return high, (x - high.astype(F32)).astype(BF16)


def three(dot, a, b):
    return dot(a[0], b[0]) + (dot(a[0], b[1]) + dot(a[1], b[0]))


def gram_kernel(
    layers, shards, pieces, chunk,
    idx_hbm, lens_hbm, own_hbm, a_hbm, g_hbm, proj_hbm,
    gram_ref, feat_ref,
    idx_ref, lens_ref, own_ref, a_ref, g_buf, proj_ref,
    acc, grad, part, part_in, both, packed, rs_in,
    in_sem, g_sem, px_send, px_recv, fx_send, fx_recv, rs_send, rs_recv,
    ag_send, ag_recv, yf_send, yf_recv, xf_send, xf_recv, cf_send, cf_recv,
):
    layer = lax.axis_index("layer")
    shard = lax.axis_index("example")
    peers = shards // 2
    spot = shard // 2
    core = shard % 2
    mate = spot * 2 + (1 - core)

    def to_layer(d):
        return ((layer + d) % layers, shard)

    def to_spot(d):
        return (layer, ((spot + d) % peers) * 2 + core)

    small = [
        pltpu.make_async_copy(src, dst, in_sem.at[i])
        for i, (src, dst) in enumerate((
            (lens_hbm, lens_ref), (own_hbm, own_ref), (a_hbm, a_ref),
            (idx_hbm, idx_ref), (proj_hbm, proj_ref),
        ))
    ]
    for load in small[:3]:
        load.start()
    loads = []
    rows = g_hbm.shape[0] // pieces
    for i in range(pieces):
        cut = pl.ds(i * rows, rows)
        load = pltpu.make_async_copy(g_hbm.at[cut], g_buf.at[cut], g_sem.at[i])
        load.start()
        loads.append(load)
    for load in small[3:]:
        load.start()

    barrier = pltpu.get_barrier_semaphore()
    targets = [to_layer(d) for d in range(1, layers)]
    targets += [to_spot(d) for d in range(1, peers)] + [(layer, mate)]
    for target in targets:
        pl.semaphore_signal(barrier, inc=1, device_id=target, device_id_type=MESH)

    for load in small[:3]:
        load.wait()
    lens = lens_ref[...].astype(F32)
    local = own_ref[...] - shard * EX_DEV
    example = lax.broadcasted_iota(jnp.int32, (EX_DEV, lens.shape[1]), 0)
    start = jnp.sum(jnp.where(local < example, lens, 0.0), axis=1, keepdims=True)
    end = jnp.sum(jnp.where(local <= example, lens, 0.0), axis=1, keepdims=True)
    rank = a_ref.shape[0]
    for i in range(pieces):
        place = (lax.broadcasted_iota(jnp.int32, (EX_DEV, rows), 1) + i * rows).astype(F32)
        mask = jnp.where((place >= start) & (place < end), 1.0, 0.0).astype(BF16)
        weighted = jnp.concatenate(
            [mask * a_ref[r : r + 1, i * rows : (i + 1) * rows] for r in range(rank)], axis=0
        )
        loads[i].wait()
        product = mm(weighted, g_buf[i * rows : (i + 1) * rows, :])
        if i == 0:
            acc[...] = product
        else:
            acc[...] += product
    width = g_hbm.shape[1] // LANES
    for r in range(rank):
        for w in range(width):
            grad[r * width + w] = acc[
                r * EX_DEV : (r + 1) * EX_DEV, w * LANES : (w + 1) * LANES
            ].astype(BF16)
    blocks, depth = proj_ref.shape[0], proj_ref.shape[1] // LANES
    for load in small[3:]:
        load.wait()
    sends = []

    def push(src, dst, send_sem, recv_sem, target):
        copy = pltpu.make_async_remote_copy(
            src_ref=src, dst_ref=dst, send_sem=send_sem, recv_sem=recv_sem,
            device_id=target, device_id_type=MESH,
        )
        copy.start()
        sends.append(copy)
        return copy

    pl.semaphore_wait(barrier, len(targets))
    copies = []
    for j in range(blocks):
        chosen = jnp.concatenate([grad[idx_ref[j, k]] for k in range(depth)], axis=1)
        part[j] = mm(chosen, proj_ref[j])
        copies.append([
            push(
                part.at[j], part_in.at[d - 1, j],
                px_send.at[d - 1, j], px_recv.at[d - 1, j], to_layer(d),
            )
            for d in range(1, layers)
        ])

    pairs = []
    for j in range(blocks):
        total = part[j]
        for d in range(1, layers):
            copies[j][d - 1].wait_recv()
            total = total + part_in[d - 1, j]
        both[0, j] = total
        pairs.append(push(both.at[0, j], both.at[1, j], fx_send.at[j], fx_recv.at[j], (layer, mate)))
    owned = EX_DEV // layers
    for j in range(blocks):
        feat_ref[:, j * LANES : (j + 1) * LANES] = both[
            0, j, pl.ds(pl.multiple_of(layer * owned, 8), owned), :
        ]
    for copy in pairs:
        copy.wait_recv()

    pair = jnp.concatenate(
        [jnp.concatenate([both[0, j], both[1, j]], axis=0) for j in range(blocks)], axis=1
    )
    high, low = split(pair)
    row = 0
    for i in range(blocks):
        cut = slice(i * LANES, (i + 1) * LANES)
        strip = three(
            mm_tn, (high[:, cut], low[:, cut]), (high[:, i * LANES :], low[:, i * LANES :])
        )
        for j in range(blocks - i):
            packed[row : row + LANES, :] = strip[:, j * LANES : (j + 1) * LANES]
            row += LANES
    if row < packed.shape[0]:
        packed[row:, :] = jnp.zeros((packed.shape[0] - row, LANES), F32)

    def where(lay, cor, spo):
        return pl.multiple_of(((lay * 2 + cor) * peers + spo) * chunk, 8)

    mine = where(layer, core, spot)
    copies = []
    for d in range(1, peers):
        source = where(layer, core, (spot + d) % peers)
        copies.append(push(
            packed.at[pl.ds(source, chunk)], rs_in.at[d - 1],
            rs_send.at[d - 1], rs_recv.at[d - 1], to_spot(d),
        ))
    total = packed[pl.ds(mine, chunk), :]
    for d in range(1, peers):
        copies[d - 1].wait_recv()
        total = total + rs_in[d - 1]
    gram_ref[pl.ds(mine, chunk), :] = total

    side = spot % 2
    line = peers // 2
    place = spot // 2
    y_mate = (layer, (place * 2 + 1 - side) * 2 + core)

    def piece(d, y):
        at = (place - d + line) % line * 2 + y
        return gram_ref.at[pl.ds(where(layer, core, at), chunk)]

    gathers = [
        push(
            piece(0, side), piece(0, side), ag_send.at[d - 1], ag_recv.at[d - 1],
            (layer, ((place + d) % line * 2 + side) * 2 + core),
        )
        for d in range(1, line)
    ]
    forwards = []

    def hand_on(d, y, flip):
        for x in range(1, layers):
            forwards.append((x, push(
                piece(d, y), piece(d, y), xf_send.at[x - 1, flip, d], xf_recv.at[x - 1, flip, d],
                to_layer(x),
            )))

    across = []
    for d in range(line):
        if d:
            gathers[d - 1].wait_recv()
        across.append(push(piece(d, side), piece(d, side), yf_send.at[d], yf_recv.at[d], y_mate))
        hand_on(d, side, 0)
        if d:
            across[d - 1].wait_recv()
            hand_on(d - 1, 1 - side, 1)
    across[line - 1].wait_recv()
    hand_on(line - 1, 1 - side, 1)
    pairs = []
    for x in range(layers):
        for way, copy in forwards:
            if way == x:
                copy.wait_recv()
        got = gram_ref.at[pl.ds(where((layer - x + layers) % layers, core, 0), peers * chunk)]
        pairs.append(push(got, got, cf_send.at[x], cf_recv.at[x], (layer, mate)))
    for copy in pairs:
        copy.wait_recv()
    for copy in sends:
        copy.wait_send()


def diagonal(shape):
    return lax.broadcasted_iota(jnp.int32, shape, 0) == lax.broadcasted_iota(jnp.int32, shape, 1)


def factor_kernel(
    scale, blocks, gram_ref, feat_ref, band_ref, white_ref,
    full, b_high, b_low, x_ref, inv, work,
):
    size = blocks * LANES
    half = size // 2
    row = 0
    for i in range(blocks):
        for j in range(i, blocks):
            block = gram_ref[row : row + LANES, :]
            row += LANES
            full[i * LANES : (i + 1) * LANES, j * LANES : (j + 1) * LANES] = block
            if j > i:
                full[j * LANES : (j + 1) * LANES, i * LANES : (i + 1) * LANES] = block.T
    gram = full[...]
    eye = diagonal((size, size))
    kept = jnp.where(eye, gram, 0.0)
    inv_row = lax.rsqrt(jnp.sum(kept, axis=0, keepdims=True))
    inv_col = lax.rsqrt(jnp.sum(kept, axis=1, keepdims=True))
    inv[...] = inv_row
    scaled = gram * inv_col * inv_row
    full[...] = scaled
    high, low = split(scaled)
    b_high[...] = high
    b_low[...] = low
    bound = jnp.max(jnp.sum(jnp.abs(scaled), axis=0, keepdims=True))
    first = 2.5 / jnp.full((1, size), bound, F32)
    rows = lax.broadcasted_iota(jnp.int32, (size, size), 0)
    cols = lax.broadcasted_iota(jnp.int32, (size, size), 1)
    root = jnp.sqrt(first)
    x_ref[...] = jnp.where(
        rows > cols, -first * scaled * root,
        jnp.where(eye, root * (1.5 - 0.5 * first * scaled), 0.0),
    )

    corner = diagonal((half, half))
    lower = lax.broadcasted_iota(jnp.int32, (half, half), 0) > lax.broadcasted_iota(
        jnp.int32, (half, half), 1
    )
    ident = jnp.where(corner, 1.0, 0.0)

    def half_low(e):
        return jnp.where(lower, e, jnp.where(corner, 0.5 * e, 0.0))

    def step(fine):
        top = x_ref[:half, :half]
        bottom = x_ref[half:, :]
        bh = b_high[...]
        if fine:
            bl = b_low[...]
            top_s, bottom_s = split(top), split(bottom)
            y0 = three(mm, top_s, (bh[:half, :half], bl[:half, :half]))
            y1 = three(mm, bottom_s, (bh, bl))
            y0_s, y1_s = split(y0), split(y1)
            e0 = three(mm_t, y0_s, top_s) - ident
            e1 = three(mm_t, (y1_s[0][:, :half], y1_s[1][:, :half]), top_s)
            e2 = three(mm_t, y1_s, bottom_s) - ident
            top_h, bottom_h = top_s[0], bottom_s[0]
        else:
            top_h, bottom_h = top.astype(BF16), bottom.astype(BF16)
            y0 = mm(top_h, bh[:half, :half]).astype(BF16)
            y1 = mm(bottom_h, bh).astype(BF16)
            e0 = mm_t(y0, top_h) - ident
            e1 = mm_t(y1[:, :half], top_h)
            e2 = mm_t(y1, bottom_h) - ident
        p0 = half_low(e0).astype(BF16)
        p1 = e1.astype(BF16)
        p2 = half_low(e2).astype(BF16)
        x_ref[:half, :half] = top - mm(p0, top_h)
        x_ref[half:, :half] = bottom[:, :half] - (mm(p1, top_h) + mm(p2, bottom_h[:, :half]))
        x_ref[half:, half:] = bottom[:, half:] - mm(p2, bottom_h[:, half:])
        return e0, e1, e2

    def norm(errors):
        e0, e1, e2 = errors
        return jnp.sum(e0 * e0 + 2.0 * (e1 * e1) + e2 * e2)

    def body(state):
        return state[0] + 1, norm(step(True))

    def blind(_, carry):
        step(False)
        return carry

    lax.fori_loop(0, 8, blind, 0)
    state = lax.while_loop(
        lambda s: (s[0] < 16) & jnp.logical_not(s[1] < 1e-4),
        body, (jnp.int32(0), F32(1e9)),
    )
    good = state[1] < 1e-4

    @pl.when(jnp.logical_not(good))
    def _():
        work[:, :size] = full[...]
        work[:, size:] = jnp.where(eye, 1.0, 0.0)
        line = lax.broadcasted_iota(jnp.int32, (1, 2 * size), 1)
        down = lax.broadcasted_iota(jnp.int32, (size, 1), 0)

        def column(j, carry):
            pivot_row = work[pl.ds(j, 1), :]
            pivot = jnp.sum(jnp.where(line == j, pivot_row, 0.0), axis=1, keepdims=True)
            pivot_row = pivot_row / jnp.sqrt(pivot)
            left = work[:, :size]
            entry = jnp.sum(jnp.where(cols == j, left, 0.0), axis=1, keepdims=True)
            entry = jnp.where(down > j, entry / jnp.sqrt(pivot), 0.0)
            work[...] = work[...] - entry * pivot_row
            work[pl.ds(j, 1), :] = pivot_row
            return carry

        lax.fori_loop(0, size, column, 0)
        x_ref[...] = jnp.where(rows >= cols, work[:, size:], 0.0)

    side = band_ref.shape[0]
    begin = pl.multiple_of(lax.axis_index("example") * side, 8)
    over = 1.0 / (inv[...] * scale)
    band_rows = lax.broadcasted_iota(jnp.int32, (side, size), 0) + begin
    upper = lax.broadcasted_iota(jnp.int32, (side, size), 1) >= band_rows

    @pl.when(good)
    def _():
        band = three(mm, split(x_ref[pl.ds(begin, side), :]), (b_high[...], b_low[...]))
        band_ref[...] = jnp.where(upper, band * over, 0.0)

    @pl.when(jnp.logical_not(good))
    def _():
        band_ref[...] = jnp.where(upper, work[pl.ds(begin, side), :size] * over, 0.0)

    white_ref[...] = scale * three(mm_t, split(feat_ref[...] * inv[...]), split(x_ref[...]))


def shards(
    adapter_input,
    output_gradient,
    projection,
    input_block_index,
    turn_token_length,
    turn_to_example,
):
    layers, count = lax.axis_size("layer"), lax.axis_size("example")
    rank, tokens = adapter_input.shape[1:]
    width = output_gradient.shape[2]
    blocks = projection.shape[1]
    size = blocks * LANES
    peers = count // 2
    pieces = 4
    packed_rows = blocks * (blocks + 1) // 2 * LANES
    owners = 2 * layers * peers
    chunk = -(-packed_rows // (owners * 8)) * 8
    vmem = pl.BlockSpec(memory_space=pltpu.VMEM)
    dma = pltpu.SemaphoreType.DMA
    near, far = max(layers - 1, 1), max(peers - 1, 1)
    gram, features = pl.pallas_call(
        functools.partial(gram_kernel, layers, count, pieces, chunk),
        out_shape=(
            jax.ShapeDtypeStruct((owners * chunk, LANES), F32),
            jax.ShapeDtypeStruct((EX_DEV // layers, size), F32),
        ),
        in_specs=[pl.BlockSpec(memory_space=pltpu.HBM)] * 6,
        out_specs=(vmem, vmem),
        scratch_shapes=[
            pltpu.SMEM(input_block_index.shape[1:], jnp.int32),
            pltpu.VMEM((1, turn_token_length.shape[0]), jnp.int32),
            pltpu.VMEM((1, turn_to_example.shape[0]), jnp.int32),
            pltpu.VMEM((rank, tokens), BF16),
            pltpu.VMEM((tokens, width), BF16),
            pltpu.VMEM(projection.shape[1:], BF16),
            pltpu.VMEM((rank * EX_DEV, width), F32),
            pltpu.VMEM((rank * width // LANES, EX_DEV, LANES), BF16),
            pltpu.VMEM((blocks, EX_DEV, LANES), F32),
            pltpu.VMEM((near, blocks, EX_DEV, LANES), F32),
            pltpu.VMEM((2, blocks, EX_DEV, LANES), F32),
            pltpu.VMEM((owners * chunk, LANES), F32),
            pltpu.VMEM((far, chunk, LANES), F32),
            dma((5,)), dma((pieces,)),
            dma((near, blocks)), dma((near, blocks)), dma((blocks,)), dma((blocks,)),
            dma((far,)), dma((far,)), dma((peers // 2,)), dma((peers // 2,)),
            dma((peers // 2,)), dma((peers // 2,)),
            dma((near, 2, peers // 2)), dma((near, 2, peers // 2)), dma((layers,)), dma((layers,)),
        ],
        compiler_params=pltpu.CompilerParams(
            collective_id=0, has_side_effects=True, vmem_limit_bytes=40 * 1024 * 1024
        ),
    )(
        input_block_index[0],
        turn_token_length.reshape(1, -1),
        turn_to_example.reshape(1, -1),
        adapter_input[0],
        output_gradient[0],
        projection[0],
    )
    return pl.pallas_call(
        functools.partial(factor_kernel, math.sqrt(EX_DEV * count), blocks),
        out_shape=(
            jax.ShapeDtypeStruct((size // count, size), F32),
            jax.ShapeDtypeStruct((EX_DEV // layers, size), F32),
        ),
        in_specs=[vmem, vmem],
        out_specs=(vmem, vmem),
        scratch_shapes=[
            pltpu.VMEM((size, size), F32),
            pltpu.VMEM((size, size), BF16),
            pltpu.VMEM((size, size), BF16),
            pltpu.VMEM((size, size), F32),
            pltpu.VMEM((1, size), F32),
            pltpu.VMEM((size, 2 * size), F32),
        ],
        compiler_params=pltpu.CompilerParams(vmem_limit_bytes=40 * 1024 * 1024),
    )(gram, features)


def solution(mesh):
    in_specs = (
        P("layer", None, "example"),
        P("layer", "example", None),
        P("layer", None, None, None),
        P("layer", None, None),
        P("example"),
        P("example"),
    )
    out_specs = (P("example", None), P(("example", "layer"), None))
    return jax.shard_map(shards, mesh=mesh, in_specs=in_specs, out_specs=out_specs, check_vma=False)
```

```python
import functools
import math

import jax
import jax.numpy as jnp
from jax import lax
from jax.experimental import pallas as pl
from jax.experimental.pallas import tpu as pltpu
from jax.sharding import PartitionSpec as P

EX_DEV = 64
LANES = 128
F32 = jnp.float32
BF16 = jnp.bfloat16
MESH = pl.DeviceIdType.MESH


def mm(a, b):
    return jnp.dot(a, b, preferred_element_type=F32)


def mm_t(a, b):
    return lax.dot_general(a, b, (((1,), (1,)), ((), ())), preferred_element_type=F32)


def mm_tn(a, b):
    return lax.dot_general(a, b, (((0,), (0,)), ((), ())), preferred_element_type=F32)


def split(x):
    high = x.astype(BF16)
    return high, (x - high.astype(F32)).astype(BF16)


def three(dot, a, b):
    return dot(a[0], b[0]) + (dot(a[0], b[1]) + dot(a[1], b[0]))


def gram_kernel(
    layers, shards, pieces, chunk,
    idx_hbm, lens_hbm, own_hbm, a_hbm, g_hbm, proj_hbm,
    gram_ref, feat_ref,
    idx_ref, lens_ref, own_ref, a_ref, g_buf, proj_ref,
    acc, grad, part, part_in, both, packed, rs_in,
    in_sem, g_sem, px_send, px_recv, fx_send, fx_recv, rs_send, rs_recv,
    ag_send, ag_recv, xf_send, xf_recv, cf_send, cf_recv,
):
    layer = lax.axis_index("layer")
    shard = lax.axis_index("example")
    peers = shards // 2
    spot = shard // 2
    core = shard % 2
    mate = spot * 2 + (1 - core)

    def to_layer(d):
        return ((layer + d) % layers, shard)

    def to_spot(d):
        return (layer, ((spot + d) % peers) * 2 + core)

    small = [
        pltpu.make_async_copy(src, dst, in_sem.at[i])
        for i, (src, dst) in enumerate((
            (lens_hbm, lens_ref), (own_hbm, own_ref), (a_hbm, a_ref),
            (idx_hbm, idx_ref), (proj_hbm, proj_ref),
        ))
    ]
    for load in small[:3]:
        load.start()
    loads = []
    rows = g_hbm.shape[0] // pieces
    for i in range(pieces):
        cut = pl.ds(i * rows, rows)
        load = pltpu.make_async_copy(g_hbm.at[cut], g_buf.at[cut], g_sem.at[i])
        load.start()
        loads.append(load)
    for load in small[3:]:
        load.start()

    barrier = pltpu.get_barrier_semaphore()
    targets = [to_layer(d) for d in range(1, layers)]
    targets += [to_spot(d) for d in range(1, peers)] + [(layer, mate)]
    for target in targets:
        pl.semaphore_signal(barrier, inc=1, device_id=target, device_id_type=MESH)

    for load in small[:3]:
        load.wait()
    lens = lens_ref[...].astype(F32)
    local = own_ref[...] - shard * EX_DEV
    example = lax.broadcasted_iota(jnp.int32, (EX_DEV, lens.shape[1]), 0)
    start = jnp.sum(jnp.where(local < example, lens, 0.0), axis=1, keepdims=True)
    end = jnp.sum(jnp.where(local <= example, lens, 0.0), axis=1, keepdims=True)
    rank = a_ref.shape[0]
    for i in range(pieces):
        place = (lax.broadcasted_iota(jnp.int32, (EX_DEV, rows), 1) + i * rows).astype(F32)
        mask = jnp.where((place >= start) & (place < end), 1.0, 0.0).astype(BF16)
        weighted = jnp.concatenate(
            [mask * a_ref[r : r + 1, i * rows : (i + 1) * rows] for r in range(rank)], axis=0
        )
        loads[i].wait()
        product = mm(weighted, g_buf[i * rows : (i + 1) * rows, :])
        if i == 0:
            acc[...] = product
        else:
            acc[...] += product
    width = g_hbm.shape[1] // LANES
    for r in range(rank):
        for w in range(width):
            grad[r * width + w] = acc[
                r * EX_DEV : (r + 1) * EX_DEV, w * LANES : (w + 1) * LANES
            ].astype(BF16)
    blocks, depth = proj_ref.shape[0], proj_ref.shape[1] // LANES
    for load in small[3:]:
        load.wait()
    sends = []

    def push(src, dst, send_sem, recv_sem, target):
        copy = pltpu.make_async_remote_copy(
            src_ref=src, dst_ref=dst, send_sem=send_sem, recv_sem=recv_sem,
            device_id=target, device_id_type=MESH,
        )
        copy.start()
        sends.append(copy)
        return copy

    pl.semaphore_wait(barrier, len(targets))
    cuts = [range(0, blocks // 2), range(blocks // 2, blocks)]
    copies = []
    for i, cut in enumerate(cuts):
        for j in cut:
            chosen = jnp.concatenate([grad[idx_ref[j, k]] for k in range(depth)], axis=1)
            part[j] = mm(chosen, proj_ref[j])
        span = pl.ds(cut[0], len(cut))
        copies.append([
            push(
                part.at[span], part_in.at[d - 1, span],
                px_send.at[d - 1, i], px_recv.at[d - 1, i], to_layer(d),
            )
            for d in range(1, layers)
        ])

    pairs = []
    for i, cut in enumerate(cuts):
        for copy in copies[i]:
            copy.wait_recv()
        for j in cut:
            total = part[j]
            for d in range(1, layers):
                total = total + part_in[d - 1, j]
            both[0, j] = total
        span = pl.ds(cut[0], len(cut))
        pairs.append(push(
            both.at[0, span], both.at[1, span], fx_send.at[i], fx_recv.at[i], (layer, mate)
        ))
    owned = EX_DEV // layers
    for j in range(blocks):
        feat_ref[:, j * LANES : (j + 1) * LANES] = both[
            0, j, pl.ds(pl.multiple_of(layer * owned, 8), owned), :
        ]
    for copy in pairs:
        copy.wait_recv()

    pair = jnp.concatenate(
        [jnp.concatenate([both[0, j], both[1, j]], axis=0) for j in range(blocks)], axis=1
    )
    high, low = split(pair)
    row = 0
    for i in range(blocks):
        cut = slice(i * LANES, (i + 1) * LANES)
        strip = three(
            mm_tn, (high[:, cut], low[:, cut]), (high[:, i * LANES :], low[:, i * LANES :])
        )
        for j in range(blocks - i):
            packed[row : row + LANES, :] = strip[:, j * LANES : (j + 1) * LANES]
            row += LANES
    if row < packed.shape[0]:
        packed[row:, :] = jnp.zeros((packed.shape[0] - row, LANES), F32)

    def where(lay, cor, spo):
        return pl.multiple_of(((lay * 2 + cor) * peers + spo) * chunk, 8)

    mine = where(layer, core, spot)
    copies = []
    for d in range(1, peers):
        source = where(layer, core, (spot + d) % peers)
        copies.append(push(
            packed.at[pl.ds(source, chunk)], rs_in.at[d - 1],
            rs_send.at[d - 1], rs_recv.at[d - 1], to_spot(d),
        ))
    total = packed[pl.ds(mine, chunk), :]
    for d in range(1, peers):
        copies[d - 1].wait_recv()
        total = total + rs_in[d - 1]
    gram_ref[pl.ds(mine, chunk), :] = total

    gathers = []
    here = gram_ref.at[pl.ds(mine, chunk)]
    for d in range(1, peers):
        gathers.append(push(here, here, ag_send.at[d - 1], ag_recv.at[d - 1], to_spot(d)))
    forwards = []
    for d in range(peers):
        if d:
            gathers[d - 1].wait_recv()
        got = gram_ref.at[pl.ds(where(layer, core, (spot - d + peers) % peers), chunk)]
        for x in range(1, layers):
            forwards.append((x, push(
                got, got, xf_send.at[x - 1, d], xf_recv.at[x - 1, d], to_layer(x)
            )))
    pairs = []
    for x in range(layers):
        for way, copy in forwards:
            if way == x:
                copy.wait_recv()
        got = gram_ref.at[pl.ds(where((layer - x + layers) % layers, core, 0), peers * chunk)]
        pairs.append(push(got, got, cf_send.at[x], cf_recv.at[x], (layer, mate)))
    for copy in pairs:
        copy.wait_recv()
    for copy in sends:
        copy.wait_send()


def diagonal(shape):
    return lax.broadcasted_iota(jnp.int32, shape, 0) == lax.broadcasted_iota(jnp.int32, shape, 1)


def factor_kernel(
    scale, blocks, gram_ref, feat_ref, band_ref, white_ref,
    full, b_high, b_low, x_ref, inv, work,
):
    size = blocks * LANES
    half = size // 2
    row = 0
    for i in range(blocks):
        for j in range(i, blocks):
            block = gram_ref[row : row + LANES, :]
            row += LANES
            full[i * LANES : (i + 1) * LANES, j * LANES : (j + 1) * LANES] = block
            if j > i:
                full[j * LANES : (j + 1) * LANES, i * LANES : (i + 1) * LANES] = block.T
    gram = full[...]
    eye = diagonal((size, size))
    kept = jnp.where(eye, gram, 0.0)
    inv_row = lax.rsqrt(jnp.sum(kept, axis=0, keepdims=True))
    inv_col = lax.rsqrt(jnp.sum(kept, axis=1, keepdims=True))
    inv[...] = inv_row
    scaled = gram * inv_col * inv_row
    full[...] = scaled
    high, low = split(scaled)
    b_high[...] = high
    b_low[...] = low
    bound = jnp.max(jnp.sum(jnp.abs(scaled), axis=0, keepdims=True))
    first = 2.5 / jnp.full((1, size), bound, F32)
    rows = lax.broadcasted_iota(jnp.int32, (size, size), 0)
    cols = lax.broadcasted_iota(jnp.int32, (size, size), 1)
    root = jnp.sqrt(first)
    x_ref[...] = jnp.where(
        rows > cols, -first * scaled * root,
        jnp.where(eye, root * (1.5 - 0.5 * first * scaled), 0.0),
    )

    corner = diagonal((half, half))
    lower = lax.broadcasted_iota(jnp.int32, (half, half), 0) > lax.broadcasted_iota(
        jnp.int32, (half, half), 1
    )
    ident = jnp.where(corner, 1.0, 0.0)

    def half_low(e):
        return jnp.where(lower, e, jnp.where(corner, 0.5 * e, 0.0))

    def step(fine):
        top = x_ref[:half, :half]
        bottom = x_ref[half:, :]
        bh = b_high[...]
        if fine:
            bl = b_low[...]
            top_s, bottom_s = split(top), split(bottom)
            y0 = three(mm, top_s, (bh[:half, :half], bl[:half, :half]))
            y1 = three(mm, bottom_s, (bh, bl))
            y0_s, y1_s = split(y0), split(y1)
            e0 = three(mm_t, y0_s, top_s) - ident
            e1 = three(mm_t, (y1_s[0][:, :half], y1_s[1][:, :half]), top_s)
            e2 = three(mm_t, y1_s, bottom_s) - ident
            top_h, bottom_h = top_s[0], bottom_s[0]
        else:
            top_h, bottom_h = top.astype(BF16), bottom.astype(BF16)
            y0 = mm(top_h, bh[:half, :half]).astype(BF16)
            y1 = mm(bottom_h, bh).astype(BF16)
            e0 = mm_t(y0, top_h) - ident
            e1 = mm_t(y1[:, :half], top_h)
            e2 = mm_t(y1, bottom_h) - ident
        p0 = half_low(e0).astype(BF16)
        p1 = e1.astype(BF16)
        p2 = half_low(e2).astype(BF16)
        x_ref[:half, :half] = top - mm(p0, top_h)
        x_ref[half:, :half] = bottom[:, :half] - (mm(p1, top_h) + mm(p2, bottom_h[:, :half]))
        x_ref[half:, half:] = bottom[:, half:] - mm(p2, bottom_h[:, half:])
        return e0, e1, e2

    def norm(errors):
        e0, e1, e2 = errors
        return jnp.sum(e0 * e0 + 2.0 * (e1 * e1) + e2 * e2)

    def body(state):
        return state[0] + 1, norm(step(True))

    def blind(_, carry):
        step(False)
        return carry

    lax.fori_loop(0, 8, blind, 0)
    state = lax.while_loop(
        lambda s: (s[0] < 16) & jnp.logical_not(s[1] < 1e-4),
        body, (jnp.int32(0), F32(1e9)),
    )
    good = state[1] < 1e-4

    @pl.when(jnp.logical_not(good))
    def _():
        work[:, :size] = full[...]
        work[:, size:] = jnp.where(eye, 1.0, 0.0)
        line = lax.broadcasted_iota(jnp.int32, (1, 2 * size), 1)
        down = lax.broadcasted_iota(jnp.int32, (size, 1), 0)

        def column(j, carry):
            pivot_row = work[pl.ds(j, 1), :]
            pivot = jnp.sum(jnp.where(line == j, pivot_row, 0.0), axis=1, keepdims=True)
            pivot_row = pivot_row / jnp.sqrt(pivot)
            left = work[:, :size]
            entry = jnp.sum(jnp.where(cols == j, left, 0.0), axis=1, keepdims=True)
            entry = jnp.where(down > j, entry / jnp.sqrt(pivot), 0.0)
            work[...] = work[...] - entry * pivot_row
            work[pl.ds(j, 1), :] = pivot_row
            return carry

        lax.fori_loop(0, size, column, 0)
        x_ref[...] = jnp.where(rows >= cols, work[:, size:], 0.0)

    side = band_ref.shape[0]
    begin = pl.multiple_of(lax.axis_index("example") * side, 8)
    over = 1.0 / (inv[...] * scale)
    band_rows = lax.broadcasted_iota(jnp.int32, (side, size), 0) + begin
    upper = lax.broadcasted_iota(jnp.int32, (side, size), 1) >= band_rows

    @pl.when(good)
    def _():
        band = three(mm, split(x_ref[pl.ds(begin, side), :]), (b_high[...], b_low[...]))
        band_ref[...] = jnp.where(upper, band * over, 0.0)

    @pl.when(jnp.logical_not(good))
    def _():
        band_ref[...] = jnp.where(upper, work[pl.ds(begin, side), :size] * over, 0.0)

    white_ref[...] = scale * three(mm_t, split(feat_ref[...] * inv[...]), split(x_ref[...]))


def shards(
    adapter_input,
    output_gradient,
    projection,
    input_block_index,
    turn_token_length,
    turn_to_example,
):
    layers, count = lax.axis_size("layer"), lax.axis_size("example")
    rank, tokens = adapter_input.shape[1:]
    width = output_gradient.shape[2]
    blocks = projection.shape[1]
    size = blocks * LANES
    peers = count // 2
    pieces = 4
    packed_rows = blocks * (blocks + 1) // 2 * LANES
    owners = 2 * layers * peers
    chunk = -(-packed_rows // (owners * 8)) * 8
    vmem = pl.BlockSpec(memory_space=pltpu.VMEM)
    dma = pltpu.SemaphoreType.DMA
    near, far = max(layers - 1, 1), max(peers - 1, 1)
    gram, features = pl.pallas_call(
        functools.partial(gram_kernel, layers, count, pieces, chunk),
        out_shape=(
            jax.ShapeDtypeStruct((owners * chunk, LANES), F32),
            jax.ShapeDtypeStruct((EX_DEV // layers, size), F32),
        ),
        in_specs=[pl.BlockSpec(memory_space=pltpu.HBM)] * 6,
        out_specs=(vmem, vmem),
        scratch_shapes=[
            pltpu.SMEM(input_block_index.shape[1:], jnp.int32),
            pltpu.VMEM((1, turn_token_length.shape[0]), jnp.int32),
            pltpu.VMEM((1, turn_to_example.shape[0]), jnp.int32),
            pltpu.VMEM((rank, tokens), BF16),
            pltpu.VMEM((tokens, width), BF16),
            pltpu.VMEM(projection.shape[1:], BF16),
            pltpu.VMEM((rank * EX_DEV, width), F32),
            pltpu.VMEM((rank * width // LANES, EX_DEV, LANES), BF16),
            pltpu.VMEM((blocks, EX_DEV, LANES), F32),
            pltpu.VMEM((near, blocks, EX_DEV, LANES), F32),
            pltpu.VMEM((2, blocks, EX_DEV, LANES), F32),
            pltpu.VMEM((owners * chunk, LANES), F32),
            pltpu.VMEM((far, chunk, LANES), F32),
            dma((5,)), dma((pieces,)),
            dma((near, 2)), dma((near, 2)), dma((2,)), dma((2,)),
            dma((far,)), dma((far,)), dma((far,)), dma((far,)),
            dma((near, peers)), dma((near, peers)), dma((layers,)), dma((layers,)),
        ],
        compiler_params=pltpu.CompilerParams(
            collective_id=0, has_side_effects=True, vmem_limit_bytes=40 * 1024 * 1024
        ),
    )(*(
        pltpu.with_memory_space_constraint(operand, pltpu.HBM)
        for operand in (
            input_block_index[0],
            turn_token_length.reshape(1, -1),
            turn_to_example.reshape(1, -1),
            adapter_input[0],
            output_gradient[0],
            projection[0],
        )
    ))
    return pl.pallas_call(
        functools.partial(factor_kernel, math.sqrt(EX_DEV * count), blocks),
        out_shape=(
            jax.ShapeDtypeStruct((size // count, size), F32),
            jax.ShapeDtypeStruct((EX_DEV // layers, size), F32),
        ),
        in_specs=[vmem, vmem],
        out_specs=(vmem, vmem),
        scratch_shapes=[
            pltpu.VMEM((size, size), F32),
            pltpu.VMEM((size, size), BF16),
            pltpu.VMEM((size, size), BF16),
            pltpu.VMEM((size, size), F32),
            pltpu.VMEM((1, size), F32),
            pltpu.VMEM((size, 2 * size), F32),
        ],
        compiler_params=pltpu.CompilerParams(vmem_limit_bytes=40 * 1024 * 1024),
    )(gram, features)


def solution(mesh):
    in_specs = (
        P("layer", None, "example"),
        P("layer", "example", None),
        P("layer", None, None, None),
        P("layer", None, None),
        P("example"),
        P("example"),
    )
    out_specs = (P("example", None), P(("example", "layer"), None))
    return jax.shard_map(shards, mesh=mesh, in_specs=in_specs, out_specs=out_specs, check_vma=False)
```

```python
import functools
import math

import jax
import jax.numpy as jnp
from jax import lax
from jax.experimental import pallas as pl
from jax.experimental.pallas import tpu as pltpu
from jax.sharding import PartitionSpec as P

EX_DEV = 64
LANES = 128
HALVES = 2
GROW = 1.5
F32 = jnp.float32
BF16 = jnp.bfloat16
MESH = pl.DeviceIdType.MESH


def mm(a, b):
    return jnp.dot(a, b, preferred_element_type=F32)


def mm_t(a, b):
    return lax.dot_general(a, b, (((1,), (1,)), ((), ())), preferred_element_type=F32)


def mm_tn(a, b):
    return lax.dot_general(a, b, (((0,), (0,)), ((), ())), preferred_element_type=F32)


def split(x):
    high = x.astype(BF16)
    return high, (x - high.astype(F32)).astype(BF16)


def three(dot, a, b):
    return dot(a[0], b[0]) + (dot(a[0], b[1]) + dot(a[1], b[0]))


def gram_kernel(
    layers, shards, pieces, chunk,
    idx_hbm, lens_hbm, own_hbm, a_hbm, g_hbm, proj_hbm,
    gram_ref, feat_ref,
    idx_ref, lens_ref, own_ref, a_ref, g_buf, proj_ref,
    w_ref, grad, part, part_in, both, packed, rs_in,
    in_sem, g_sem, px_send, px_recv, fx_send, fx_recv, rs_send, rs_recv,
    ag_send, ag_recv, xf_send, xf_recv, cf_send, cf_recv,
):
    layer = lax.axis_index("layer")
    shard = lax.axis_index("example")
    peers = shards // 2
    spot = shard // 2
    core = shard % 2
    mate = spot * 2 + (1 - core)

    def to_layer(d):
        return ((layer + d) % layers, shard)

    def to_spot(d):
        return (layer, ((spot + d) % peers) * 2 + core)

    small = [
        pltpu.make_async_copy(src, dst, in_sem.at[i])
        for i, (src, dst) in enumerate((
            (lens_hbm, lens_ref), (own_hbm, own_ref), (a_hbm, a_ref),
            (idx_hbm, idx_ref), (proj_hbm, proj_ref),
        ))
    ]
    for load in small[:3]:
        load.start()
    loads = []
    rows = g_hbm.shape[0] // pieces
    for i in range(pieces):
        cut = pl.ds(i * rows, rows)
        load = pltpu.make_async_copy(g_hbm.at[cut], g_buf.at[cut], g_sem.at[i])
        load.start()
        loads.append(load)
    for load in small[3:]:
        load.start()

    barrier = pltpu.get_barrier_semaphore()
    targets = [to_layer(d) for d in range(1, layers)]
    targets += [to_spot(d) for d in range(1, peers)] + [(layer, mate)]
    for target in targets:
        pl.semaphore_signal(barrier, inc=1, device_id=target, device_id_type=MESH)

    for load in small[:3]:
        load.wait()
    lens = lens_ref[...].astype(F32)
    local = own_ref[...] - shard * EX_DEV
    example = lax.broadcasted_iota(jnp.int32, (EX_DEV, lens.shape[1]), 0)
    start = jnp.sum(jnp.where(local < example, lens, 0.0), axis=1, keepdims=True)
    end = jnp.sum(jnp.where(local <= example, lens, 0.0), axis=1, keepdims=True)
    rank, tokens = a_ref.shape
    some = EX_DEV // HALVES
    for i in range(pieces):
        span = slice(i * rows, (i + 1) * rows)
        place = (lax.broadcasted_iota(jnp.int32, (EX_DEV, rows), 1) + i * rows).astype(F32)
        mask = jnp.where((place >= start) & (place < end), 1.0, 0.0).astype(BF16)
        for h in range(HALVES):
            for r in range(rank):
                w_ref[(h * rank + r) * some : (h * rank + r + 1) * some, span] = (
                    mask[h * some : (h + 1) * some] * a_ref[r : r + 1, span]
                )
    for load in loads:
        load.wait()
    for load in small[3:]:
        load.wait()
    sends = []

    def push(src, dst, send_sem, recv_sem, target):
        copy = pltpu.make_async_remote_copy(
            src_ref=src, dst_ref=dst, send_sem=send_sem, recv_sem=recv_sem,
            device_id=target, device_id_type=MESH,
        )
        copy.start()
        sends.append(copy)
        return copy

    width = g_hbm.shape[1] // LANES
    blocks, depth = proj_ref.shape[0], proj_ref.shape[1] // LANES
    copies = []
    for h in range(HALVES):
        summed = mm(w_ref[h * rank * some : (h + 1) * rank * some, :], g_buf[...])
        for r in range(rank):
            for w in range(width):
                grad[h, r * width + w] = summed[
                    r * some : (r + 1) * some, w * LANES : (w + 1) * LANES
                ].astype(BF16)
        cut = pl.ds(h * some, some)
        for j in range(blocks):
            chosen = jnp.concatenate([grad[h, idx_ref[j, k]] for k in range(depth)], axis=1)
            part[cut, j * LANES : (j + 1) * LANES] = mm(chosen, proj_ref[j])
        if h == 0:
            pl.semaphore_wait(barrier, len(targets))
        copies.append([
            push(
                part.at[cut], part_in.at[d - 1, cut],
                px_send.at[d - 1, h], px_recv.at[d - 1, h], to_layer(d),
            )
            for d in range(1, layers)
        ])

    pairs = []
    for h in range(HALVES):
        cut = pl.ds(h * some, some)
        total = part[cut, :]
        for d in range(1, layers):
            copies[h][d - 1].wait_recv()
            total = total + part_in[d - 1, cut, :]
        both[0, cut, :] = total
        pairs.append(push(
            both.at[0, cut], both.at[1, cut], fx_send.at[h], fx_recv.at[h], (layer, mate)
        ))
    owned = EX_DEV // layers
    feat_ref[...] = both[0, pl.ds(pl.multiple_of(layer * owned, 8), owned), :]
    for copy in pairs:
        copy.wait_recv()

    high, low = split(jnp.concatenate([both[0], both[1]], axis=0))
    row = 0
    for i in range(blocks):
        cut = slice(i * LANES, (i + 1) * LANES)
        strip = three(
            mm_tn, (high[:, cut], low[:, cut]), (high[:, i * LANES :], low[:, i * LANES :])
        )
        for j in range(blocks - i):
            packed[row : row + LANES, :] = strip[:, j * LANES : (j + 1) * LANES]
            row += LANES
    if row < packed.shape[0]:
        packed[row:, :] = jnp.zeros((packed.shape[0] - row, LANES), F32)

    def where(lay, cor, spo):
        return pl.multiple_of(((lay * 2 + cor) * peers + spo) * chunk, 8)

    mine = where(layer, core, spot)
    copies = []
    for d in range(1, peers):
        source = where(layer, core, (spot + d) % peers)
        copies.append(push(
            packed.at[pl.ds(source, chunk)], rs_in.at[d - 1],
            rs_send.at[d - 1], rs_recv.at[d - 1], to_spot(d),
        ))
    total = packed[pl.ds(mine, chunk), :]
    for d in range(1, peers):
        copies[d - 1].wait_recv()
        total = total + rs_in[d - 1]
    gram_ref[pl.ds(mine, chunk), :] = total

    gathers = []
    here = gram_ref.at[pl.ds(mine, chunk)]
    for d in range(1, peers):
        gathers.append(push(here, here, ag_send.at[d - 1], ag_recv.at[d - 1], to_spot(d)))
    forwards = []
    for d in range(peers):
        if d:
            gathers[d - 1].wait_recv()
        got = gram_ref.at[pl.ds(where(layer, core, (spot - d + peers) % peers), chunk)]
        for x in range(1, layers):
            forwards.append((x, push(
                got, got, xf_send.at[x - 1, d], xf_recv.at[x - 1, d], to_layer(x)
            )))
    pairs = []
    for x in range(layers):
        for way, copy in forwards:
            if way == x:
                copy.wait_recv()
        got = gram_ref.at[pl.ds(where((layer - x + layers) % layers, core, 0), peers * chunk)]
        pairs.append(push(got, got, cf_send.at[x], cf_recv.at[x], (layer, mate)))
    for copy in pairs:
        copy.wait_recv()
    for copy in sends:
        copy.wait_send()


def diagonal(shape):
    return lax.broadcasted_iota(jnp.int32, shape, 0) == lax.broadcasted_iota(jnp.int32, shape, 1)


def factor_kernel(
    scale, blocks, gram_ref, feat_ref, band_ref, white_ref,
    full, b_high, b_low, x_ref, coarse, inv, work,
):
    size = blocks * LANES
    half = size // 2
    row = 0
    for i in range(blocks):
        for j in range(i, blocks):
            block = gram_ref[row : row + LANES, :]
            row += LANES
            full[i * LANES : (i + 1) * LANES, j * LANES : (j + 1) * LANES] = block
            if j > i:
                full[j * LANES : (j + 1) * LANES, i * LANES : (i + 1) * LANES] = block.T
    gram = full[...]
    eye = diagonal((size, size))
    kept = jnp.where(eye, gram, 0.0)
    inv_row = lax.rsqrt(jnp.sum(kept, axis=0, keepdims=True))
    inv_col = lax.rsqrt(jnp.sum(kept, axis=1, keepdims=True))
    inv[...] = inv_row
    scaled = gram * inv_col * inv_row
    full[...] = scaled
    high, low = split(scaled)
    b_high[...] = high
    b_low[...] = low
    bound = jnp.max(jnp.sum(jnp.abs(scaled), axis=0, keepdims=True))
    first = 2.5 / jnp.full((1, size), bound, F32)
    rows = lax.broadcasted_iota(jnp.int32, (size, size), 0)
    cols = lax.broadcasted_iota(jnp.int32, (size, size), 1)
    root = jnp.sqrt(first * GROW)
    coarse[...] = jnp.where(
        rows > cols, -first * scaled * root,
        jnp.where(eye, root * (1.5 - 0.5 * first * scaled), 0.0),
    ).astype(BF16)

    corner = diagonal((half, half))
    lower = lax.broadcasted_iota(jnp.int32, (half, half), 0) > lax.broadcasted_iota(
        jnp.int32, (half, half), 1
    )
    ident = jnp.where(corner, 1.0, 0.0)

    def half_low(e):
        return jnp.where(lower, e, jnp.where(corner, 0.5 * e, 0.0))

    def update(e0, e1, e2, top_h, bottom_h):
        p0 = half_low(e0).astype(BF16)
        p1 = e1.astype(BF16)
        p2 = half_low(e2).astype(BF16)
        return (
            mm(p0, top_h),
            mm(p1, top_h) + mm(p2, bottom_h[:, :half]),
            mm(p2, bottom_h[:, half:]),
        )

    def blind(grow):
        top, bottom = coarse[:half, :half], coarse[half:, :]
        y0 = mm(top, b_high[:half, :half]).astype(BF16)
        y1 = mm(bottom, b_high[...]).astype(BF16)
        e0 = mm_t(y0, top) - ident
        e1 = mm_t(y1[:, :half], top)
        e2 = mm_t(y1, bottom) - ident
        d0, d1, d2 = update(e0, e1, e2, top, bottom)
        bottom = bottom.astype(F32)
        coarse[:half, :half] = ((top.astype(F32) - d0) * grow).astype(BF16)
        coarse[half:, :half] = ((bottom[:, :half] - d1) * grow).astype(BF16)
        coarse[half:, half:] = ((bottom[:, half:] - d2) * grow).astype(BF16)

    def middle():
        top, bottom = coarse[:half, :half], coarse[half:, :]
        y0 = split(mm(top, b_high[:half, :half]) + mm(top, b_low[:half, :half]))
        y1 = split(mm(bottom, b_high[...]) + mm(bottom, b_low[...]))
        e0 = mm_t(y0[0], top) + mm_t(y0[1], top) - ident
        e1 = mm_t(y1[0][:, :half], top) + mm_t(y1[1][:, :half], top)
        e2 = mm_t(y1[0], bottom) + mm_t(y1[1], bottom) - ident
        d0, d1, d2 = update(e0, e1, e2, top, bottom)
        x_ref[:half, :half] = top.astype(F32) - d0
        x_ref[:half, half:] = jnp.zeros((half, half), F32)
        x_ref[half:, :half] = bottom[:, :half].astype(F32) - d1
        x_ref[half:, half:] = bottom[:, half:].astype(F32) - d2

    def fine():
        top, bottom = x_ref[:half, :half], x_ref[half:, :]
        top_s, bottom_s = split(top), split(bottom)
        y0 = split(three(mm, top_s, (b_high[:half, :half], b_low[:half, :half])))
        y1 = split(three(mm, bottom_s, (b_high[...], b_low[...])))
        e0 = three(mm_t, y0, top_s) - ident
        e1 = three(mm_t, (y1[0][:, :half], y1[1][:, :half]), top_s)
        e2 = three(mm_t, y1, bottom_s) - ident
        d0, d1, d2 = update(e0, e1, e2, top_s[0], bottom_s[0])
        x_ref[:half, :half] = top - d0
        x_ref[half:, :half] = bottom[:, :half] - d1
        x_ref[half:, half:] = bottom[:, half:] - d2
        return e0, e1, e2

    def norm(errors):
        e0, e1, e2 = errors
        return jnp.sum(e0 * e0 + 2.0 * (e1 * e1) + e2 * e2)

    def body(state):
        return state[0] + 1, norm(fine())

    def blind_step(grow, _, carry):
        blind(grow)
        return carry

    lax.fori_loop(0, 3, functools.partial(blind_step, math.sqrt(GROW)), 0)
    lax.fori_loop(0, 3, functools.partial(blind_step, 1.0), 0)
    middle()
    state = lax.while_loop(
        lambda s: (s[0] < 16) & jnp.logical_not(s[1] < 1e-4),
        body, (jnp.int32(0), F32(1e9)),
    )
    good = state[1] < 1e-4

    @pl.when(jnp.logical_not(good))
    def _():
        work[:, :size] = full[...]
        work[:, size:] = jnp.where(eye, 1.0, 0.0)
        line = lax.broadcasted_iota(jnp.int32, (1, 2 * size), 1)
        down = lax.broadcasted_iota(jnp.int32, (size, 1), 0)

        def column(j, carry):
            pivot_row = work[pl.ds(j, 1), :]
            pivot = jnp.sum(jnp.where(line == j, pivot_row, 0.0), axis=1, keepdims=True)
            pivot_row = pivot_row / jnp.sqrt(pivot)
            left = work[:, :size]
            entry = jnp.sum(jnp.where(cols == j, left, 0.0), axis=1, keepdims=True)
            entry = jnp.where(down > j, entry / jnp.sqrt(pivot), 0.0)
            work[...] = work[...] - entry * pivot_row
            work[pl.ds(j, 1), :] = pivot_row
            return carry

        lax.fori_loop(0, size, column, 0)
        x_ref[...] = jnp.where(rows >= cols, work[:, size:], 0.0)

    side = band_ref.shape[0]
    begin = pl.multiple_of(lax.axis_index("example") * side, 8)
    over = 1.0 / (inv[...] * scale)
    band_rows = lax.broadcasted_iota(jnp.int32, (side, size), 0) + begin
    upper = lax.broadcasted_iota(jnp.int32, (side, size), 1) >= band_rows

    @pl.when(good)
    def _():
        band = three(mm, split(x_ref[pl.ds(begin, side), :]), (b_high[...], b_low[...]))
        band_ref[...] = jnp.where(upper, band * over, 0.0)

    @pl.when(jnp.logical_not(good))
    def _():
        band_ref[...] = jnp.where(upper, work[pl.ds(begin, side), :size] * over, 0.0)

    white_ref[...] = scale * three(mm_t, split(feat_ref[...] * inv[...]), split(x_ref[...]))


def shards(
    adapter_input,
    output_gradient,
    projection,
    input_block_index,
    turn_token_length,
    turn_to_example,
):
    layers, count = lax.axis_size("layer"), lax.axis_size("example")
    rank, tokens = adapter_input.shape[1:]
    width = output_gradient.shape[2]
    blocks = projection.shape[1]
    size = blocks * LANES
    peers = count // 2
    pieces = 4
    packed_rows = blocks * (blocks + 1) // 2 * LANES
    owners = 2 * layers * peers
    chunk = -(-packed_rows // (owners * 8)) * 8
    vmem = pl.BlockSpec(memory_space=pltpu.VMEM)
    dma = pltpu.SemaphoreType.DMA
    near, far = max(layers - 1, 1), max(peers - 1, 1)
    gram, features = pl.pallas_call(
        functools.partial(gram_kernel, layers, count, pieces, chunk),
        out_shape=(
            jax.ShapeDtypeStruct((owners * chunk, LANES), F32),
            jax.ShapeDtypeStruct((EX_DEV // layers, size), F32),
        ),
        in_specs=[pl.BlockSpec(memory_space=pltpu.HBM)] * 6,
        out_specs=(vmem, vmem),
        scratch_shapes=[
            pltpu.SMEM(input_block_index.shape[1:], jnp.int32),
            pltpu.VMEM((1, turn_token_length.shape[0]), jnp.int32),
            pltpu.VMEM((1, turn_to_example.shape[0]), jnp.int32),
            pltpu.VMEM((rank, tokens), BF16),
            pltpu.VMEM((tokens, width), BF16),
            pltpu.VMEM(projection.shape[1:], BF16),
            pltpu.VMEM((rank * EX_DEV, tokens), BF16),
            pltpu.VMEM((HALVES, rank * width // LANES, EX_DEV // HALVES, LANES), BF16),
            pltpu.VMEM((EX_DEV, size), F32),
            pltpu.VMEM((near, EX_DEV, size), F32),
            pltpu.VMEM((2, EX_DEV, size), F32),
            pltpu.VMEM((owners * chunk, LANES), F32),
            pltpu.VMEM((far, chunk, LANES), F32),
            dma((5,)), dma((pieces,)),
            dma((near, HALVES)), dma((near, HALVES)), dma((HALVES,)), dma((HALVES,)),
            dma((far,)), dma((far,)), dma((far,)), dma((far,)),
            dma((near, peers)), dma((near, peers)), dma((layers,)), dma((layers,)),
        ],
        compiler_params=pltpu.CompilerParams(
            collective_id=0, has_side_effects=True, vmem_limit_bytes=40 * 1024 * 1024
        ),
    )(*(
        pltpu.with_memory_space_constraint(operand, pltpu.HBM)
        for operand in (
            input_block_index[0],
            turn_token_length.reshape(1, -1),
            turn_to_example.reshape(1, -1),
            adapter_input[0],
            output_gradient[0],
            projection[0],
        )
    ))
    return pl.pallas_call(
        functools.partial(factor_kernel, math.sqrt(EX_DEV * count), blocks),
        out_shape=(
            jax.ShapeDtypeStruct((size // count, size), F32),
            jax.ShapeDtypeStruct((EX_DEV // layers, size), F32),
        ),
        in_specs=[vmem, vmem],
        out_specs=(vmem, vmem),
        scratch_shapes=[
            pltpu.VMEM((size, size), F32),
            pltpu.VMEM((size, size), BF16),
            pltpu.VMEM((size, size), BF16),
            pltpu.VMEM((size, size), F32),
            pltpu.VMEM((size, size), BF16),
            pltpu.VMEM((1, size), F32),
            pltpu.VMEM((size, 2 * size), F32),
        ],
        compiler_params=pltpu.CompilerParams(vmem_limit_bytes=40 * 1024 * 1024),
    )(gram, features)


def solution(mesh):
    in_specs = (
        P("layer", None, "example"),
        P("layer", "example", None),
        P("layer", None, None, None),
        P("layer", None, None),
        P("example"),
        P("example"),
    )
    out_specs = (P("example", None), P(("example", "layer"), None))
    return jax.shard_map(shards, mesh=mesh, in_specs=in_specs, out_specs=out_specs, check_vma=False)
```

```python
import functools
import math

import jax
import jax.numpy as jnp
from jax import lax
from jax.experimental import pallas as pl
from jax.experimental.pallas import tpu as pltpu
from jax.sharding import PartitionSpec as P

EX_DEV = 64
LANES = 128
HALVES = 2
GROW = 1.5
F32 = jnp.float32
BF16 = jnp.bfloat16
MESH = pl.DeviceIdType.MESH


def mm(a, b):
    return jnp.dot(a, b, preferred_element_type=F32)


def mm_t(a, b):
    return lax.dot_general(a, b, (((1,), (1,)), ((), ())), preferred_element_type=F32)


def mm_tn(a, b):
    return lax.dot_general(a, b, (((0,), (0,)), ((), ())), preferred_element_type=F32)


def split(x):
    high = x.astype(BF16)
    return high, (x - high.astype(F32)).astype(BF16)


def three(dot, a, b):
    return dot(a[0], b[0]) + (dot(a[0], b[1]) + dot(a[1], b[0]))


def gram_kernel(
    layers, shards, pieces, chunk,
    idx_hbm, lens_hbm, own_hbm, a_hbm, g_hbm, proj_hbm,
    gram_ref, feat_ref,
    idx_ref, lens_ref, own_ref, a_ref, g_buf, proj_ref,
    w_ref, grad, part, part_in, both, packed, rs_in,
    in_sem, g_sem, px_send, px_recv, fx_send, fx_recv, rs_send, rs_recv,
    ag_send, ag_recv, xf_send, xf_recv, cf_send, cf_recv,
):
    layer = lax.axis_index("layer")
    shard = lax.axis_index("example")
    peers = shards // 2
    spot = shard // 2
    core = shard % 2
    mate = spot * 2 + (1 - core)

    def to_layer(d):
        return ((layer + d) % layers, shard)

    def to_spot(d):
        return (layer, ((spot + d) % peers) * 2 + core)

    small = [
        pltpu.make_async_copy(src, dst, in_sem.at[i])
        for i, (src, dst) in enumerate((
            (lens_hbm, lens_ref), (own_hbm, own_ref), (a_hbm, a_ref),
            (idx_hbm, idx_ref), (proj_hbm, proj_ref),
        ))
    ]
    for load in small[:3]:
        load.start()
    loads = []
    rows = g_hbm.shape[0] // pieces
    for i in range(pieces):
        cut = pl.ds(i * rows, rows)
        load = pltpu.make_async_copy(g_hbm.at[cut], g_buf.at[cut], g_sem.at[i])
        load.start()
        loads.append(load)
    for load in small[3:]:
        load.start()

    barrier = pltpu.get_barrier_semaphore()
    targets = [to_layer(d) for d in range(1, layers)]
    targets += [to_spot(d) for d in range(1, peers)] + [(layer, mate)]
    for target in targets:
        pl.semaphore_signal(barrier, inc=1, device_id=target, device_id_type=MESH)

    for load in small[:3]:
        load.wait()
    lens = lens_ref[...].astype(F32)
    local = own_ref[...] - shard * EX_DEV
    example = lax.broadcasted_iota(jnp.int32, (EX_DEV, lens.shape[1]), 0)
    start = jnp.sum(jnp.where(local < example, lens, 0.0), axis=1, keepdims=True)
    end = jnp.sum(jnp.where(local <= example, lens, 0.0), axis=1, keepdims=True)
    rank, tokens = a_ref.shape
    some = EX_DEV // HALVES
    for i in range(pieces):
        span = slice(i * rows, (i + 1) * rows)
        place = (lax.broadcasted_iota(jnp.int32, (EX_DEV, rows), 1) + i * rows).astype(F32)
        mask = jnp.where((place >= start) & (place < end), 1.0, 0.0).astype(BF16)
        for h in range(HALVES):
            for r in range(rank):
                w_ref[(h * rank + r) * some : (h * rank + r + 1) * some, span] = (
                    mask[h * some : (h + 1) * some] * a_ref[r : r + 1, span]
                )
    for load in loads:
        load.wait()
    for load in small[3:]:
        load.wait()
    sends = []

    def push(src, dst, send_sem, recv_sem, target):
        copy = pltpu.make_async_remote_copy(
            src_ref=src, dst_ref=dst, send_sem=send_sem, recv_sem=recv_sem,
            device_id=target, device_id_type=MESH,
        )
        copy.start()
        sends.append(copy)
        return copy

    width = g_hbm.shape[1] // LANES
    blocks, depth = proj_ref.shape[0], proj_ref.shape[1] // LANES
    copies = []
    for h in range(HALVES):
        summed = mm(w_ref[h * rank * some : (h + 1) * rank * some, :], g_buf[...])
        for r in range(rank):
            for w in range(width):
                grad[h, r * width + w] = summed[
                    r * some : (r + 1) * some, w * LANES : (w + 1) * LANES
                ].astype(BF16)
        cut = pl.ds(h * some, some)
        for j in range(blocks):
            chosen = jnp.concatenate([grad[h, idx_ref[j, k]] for k in range(depth)], axis=1)
            part[cut, j * LANES : (j + 1) * LANES] = mm(chosen, proj_ref[j])
        if h == 0:
            pl.semaphore_wait(barrier, len(targets))
        copies.append([
            push(
                part.at[cut], part_in.at[d - 1, cut],
                px_send.at[d - 1, h], px_recv.at[d - 1, h], to_layer(d),
            )
            for d in range(1, layers)
        ])

    pairs = []
    for h in range(HALVES):
        cut = pl.ds(h * some, some)
        total = part[cut, :]
        for d in range(1, layers):
            copies[h][d - 1].wait_recv()
            total = total + part_in[d - 1, cut, :]
        both[0, cut, :] = total
        pairs.append(push(
            both.at[0, cut], both.at[1, cut], fx_send.at[h], fx_recv.at[h], (layer, mate)
        ))
    owned = EX_DEV // layers
    feat_ref[...] = both[0, pl.ds(pl.multiple_of(layer * owned, 8), owned), :]
    for copy in pairs:
        copy.wait_recv()

    high, low = split(jnp.concatenate([both[0], both[1]], axis=0))
    left = jnp.concatenate([high, high, low], axis=0)
    right = jnp.concatenate([high, low, high], axis=0)
    row = 0
    for i in range(blocks):
        cut = slice(i * LANES, (i + 1) * LANES)
        strip = mm_tn(left[:, cut], right[:, i * LANES :])
        for j in range(blocks - i):
            packed[row : row + LANES, :] = strip[:, j * LANES : (j + 1) * LANES]
            row += LANES
    if row < packed.shape[0]:
        packed[row:, :] = jnp.zeros((packed.shape[0] - row, LANES), F32)

    def where(lay, cor, spo):
        return pl.multiple_of(((lay * 2 + cor) * peers + spo) * chunk, 8)

    mine = where(layer, core, spot)
    copies = []
    for d in range(1, peers):
        source = where(layer, core, (spot + d) % peers)
        copies.append(push(
            packed.at[pl.ds(source, chunk)], rs_in.at[d - 1],
            rs_send.at[d - 1], rs_recv.at[d - 1], to_spot(d),
        ))
    total = packed[pl.ds(mine, chunk), :]
    for d in range(1, peers):
        copies[d - 1].wait_recv()
        total = total + rs_in[d - 1]
    gram_ref[pl.ds(mine, chunk), :] = total

    gathers = []
    here = gram_ref.at[pl.ds(mine, chunk)]
    for d in range(1, peers):
        gathers.append(push(here, here, ag_send.at[d - 1], ag_recv.at[d - 1], to_spot(d)))
    forwards = []
    for d in range(peers):
        if d:
            gathers[d - 1].wait_recv()
        got = gram_ref.at[pl.ds(where(layer, core, (spot - d + peers) % peers), chunk)]
        for x in range(1, layers):
            forwards.append((x, push(
                got, got, xf_send.at[x - 1, d], xf_recv.at[x - 1, d], to_layer(x)
            )))
    pairs = []
    for x in range(layers):
        for way, copy in forwards:
            if way == x:
                copy.wait_recv()
        got = gram_ref.at[pl.ds(where((layer - x + layers) % layers, core, 0), peers * chunk)]
        pairs.append(push(got, got, cf_send.at[x], cf_recv.at[x], (layer, mate)))
    for copy in pairs:
        copy.wait_recv()
    for copy in sends:
        copy.wait_send()


def diagonal(shape):
    return lax.broadcasted_iota(jnp.int32, shape, 0) == lax.broadcasted_iota(jnp.int32, shape, 1)


def factor_kernel(
    scale, blocks, gram_ref, feat_ref, band_ref, white_ref,
    full, b_high, b_low, x_ref, coarse, inv, work,
):
    size = blocks * LANES
    half = size // 2
    row = 0
    for i in range(blocks):
        for j in range(i, blocks):
            block = gram_ref[row : row + LANES, :]
            row += LANES
            full[i * LANES : (i + 1) * LANES, j * LANES : (j + 1) * LANES] = block
            if j > i:
                full[j * LANES : (j + 1) * LANES, i * LANES : (i + 1) * LANES] = block.T
    gram = full[...]
    eye = diagonal((size, size))
    kept = jnp.where(eye, gram, 0.0)
    inv_row = lax.rsqrt(jnp.sum(kept, axis=0, keepdims=True))
    inv_col = lax.rsqrt(jnp.sum(kept, axis=1, keepdims=True))
    inv[...] = inv_row
    scaled = gram * inv_col * inv_row
    full[...] = scaled
    high, low = split(scaled)
    b_high[...] = high
    b_low[...] = low
    bound = jnp.max(jnp.sum(jnp.abs(scaled), axis=0, keepdims=True))
    first = 2.5 / jnp.full((1, size), bound, F32)
    rows = lax.broadcasted_iota(jnp.int32, (size, size), 0)
    cols = lax.broadcasted_iota(jnp.int32, (size, size), 1)
    root = jnp.sqrt(first * GROW)
    coarse[...] = jnp.where(
        rows > cols, -first * scaled * root,
        jnp.where(eye, root * (1.5 - 0.5 * first * scaled), 0.0),
    ).astype(BF16)

    corner = diagonal((half, half))
    lower = lax.broadcasted_iota(jnp.int32, (half, half), 0) > lax.broadcasted_iota(
        jnp.int32, (half, half), 1
    )
    ident = jnp.where(corner, 1.0, 0.0)

    def half_low(e):
        return jnp.where(lower, e, jnp.where(corner, 0.5 * e, 0.0))

    def update(e0, e1, e2, top_h, bottom_h):
        p0 = half_low(e0).astype(BF16)
        p1 = e1.astype(BF16)
        p2 = half_low(e2).astype(BF16)
        return (
            mm(p0, top_h),
            mm(p1, top_h) + mm(p2, bottom_h[:, :half]),
            mm(p2, bottom_h[:, half:]),
        )

    def norm(errors):
        e0, e1, e2 = errors
        return jnp.sum(e0 * e0 + 2.0 * (e1 * e1) + e2 * e2)

    def blind(grow):
        top, bottom = coarse[:half, :half], coarse[half:, :]
        y0 = mm(top, b_high[:half, :half]).astype(BF16)
        y1 = mm(bottom, b_high[...]).astype(BF16)
        e0 = mm_t(y0, top) - ident
        e1 = mm_t(y1[:, :half], top)
        e2 = mm_t(y1, bottom) - ident
        d0, d1, d2 = update(e0, e1, e2, top, bottom)
        bottom = bottom.astype(F32)
        coarse[:half, :half] = ((top.astype(F32) - d0) * grow).astype(BF16)
        coarse[half:, :half] = ((bottom[:, :half] - d1) * grow).astype(BF16)
        coarse[half:, half:] = ((bottom[:, half:] - d2) * grow).astype(BF16)

    def middle():
        top, bottom = coarse[:half, :half], coarse[half:, :]
        y0 = split(mm(top, b_high[:half, :half]) + mm(top, b_low[:half, :half]))
        y1 = split(mm(bottom, b_high[...]) + mm(bottom, b_low[...]))
        e0 = mm_t(y0[0], top) + mm_t(y0[1], top) - ident
        e1 = mm_t(y1[0][:, :half], top) + mm_t(y1[1][:, :half], top)
        e2 = mm_t(y1[0], bottom) + mm_t(y1[1], bottom) - ident
        l0, l1, l2 = half_low(e0), e1, half_low(e2)
        p0, p1, p2 = l0.astype(BF16), l1.astype(BF16), l2.astype(BF16)
        g0, g1, g2 = e0.astype(BF16), e1.astype(BF16), e2.astype(BF16)
        m00, m01 = mm(p0, g0), mm_t(p0, g1)
        m10 = mm(p1, g0) + mm(p2, g1)
        m11 = mm_t(p1, g1) + mm(p2, g2)
        n00 = (p0.astype(F32) + m00).astype(BF16)
        n10 = (p1.astype(F32) + m10).astype(BF16)
        n11 = (p2.astype(F32) + m11).astype(BF16)
        k0, k2 = e0 - p0.astype(F32) - m00, e2 - p2.astype(F32) - m11
        k0 = k0 - (p0.astype(F32) + m00).T + mm_t(n00, p0)
        k1 = e1 - p1.astype(F32) - m10 - m01.T + mm_t(n10, p0)
        k2 = k2 - (p2.astype(F32) + m11).T + mm_t(n10, p1) + mm_t(n11, p2)
        d0, d1, d2 = mm(p0, top), mm(p1, top) + mm(p2, bottom[:, :half]), mm(p2, bottom[:, half:])
        x0 = top.astype(F32) - d0
        x1 = bottom[:, :half].astype(F32) - d1
        x2 = bottom[:, half:].astype(F32) - d2
        x1_h = jnp.concatenate([x1.astype(BF16), x2.astype(BF16)], axis=1)
        d0, d1, d2 = update(k0, k1, k2, x0.astype(BF16), x1_h)
        x_ref[:half, :half] = x0 - d0
        x_ref[:half, half:] = jnp.zeros((half, half), F32)
        x_ref[half:, :half] = x1 - d1
        x_ref[half:, half:] = x2 - d2
        return norm((k0, k1, k2)), norm((e0, e1, e2))

    def fine():
        top, bottom = x_ref[:half, :half], x_ref[half:, :]
        top_s, bottom_s = split(top), split(bottom)
        y0 = split(three(mm, top_s, (b_high[:half, :half], b_low[:half, :half])))
        y1 = split(three(mm, bottom_s, (b_high[...], b_low[...])))
        e0 = three(mm_t, y0, top_s) - ident
        e1 = three(mm_t, (y1[0][:, :half], y1[1][:, :half]), top_s)
        e2 = three(mm_t, y1, bottom_s) - ident
        d0, d1, d2 = update(e0, e1, e2, top_s[0], bottom_s[0])
        x_ref[:half, :half] = top - d0
        x_ref[half:, :half] = bottom[:, :half] - d1
        x_ref[half:, half:] = bottom[:, half:] - d2
        return e0, e1, e2

    def body(state):
        return state[0] + 1, norm(fine())

    def blind_step(grow, _, carry):
        blind(grow)
        return carry

    lax.fori_loop(0, 3, functools.partial(blind_step, math.sqrt(GROW)), 0)
    lax.fori_loop(0, 3, functools.partial(blind_step, 1.0), 0)
    error, before = middle()
    near = (error < 1e-4) & (before < 1.0)
    state = lax.while_loop(
        lambda s: (s[0] < 16) & jnp.logical_not(s[1] < 1e-4),
        body, (jnp.int32(0), jnp.where(near, error, 1e9)),
    )
    good = state[1] < 1e-4

    @pl.when(jnp.logical_not(good))
    def _():
        work[:, :size] = full[...]
        work[:, size:] = jnp.where(eye, 1.0, 0.0)
        line = lax.broadcasted_iota(jnp.int32, (1, 2 * size), 1)
        down = lax.broadcasted_iota(jnp.int32, (size, 1), 0)

        def column(j, carry):
            pivot_row = work[pl.ds(j, 1), :]
            pivot = jnp.sum(jnp.where(line == j, pivot_row, 0.0), axis=1, keepdims=True)
            pivot_row = pivot_row / jnp.sqrt(pivot)
            left = work[:, :size]
            entry = jnp.sum(jnp.where(cols == j, left, 0.0), axis=1, keepdims=True)
            entry = jnp.where(down > j, entry / jnp.sqrt(pivot), 0.0)
            work[...] = work[...] - entry * pivot_row
            work[pl.ds(j, 1), :] = pivot_row
            return carry

        lax.fori_loop(0, size, column, 0)
        x_ref[...] = jnp.where(rows >= cols, work[:, size:], 0.0)

    side = band_ref.shape[0]
    begin = pl.multiple_of(lax.axis_index("example") * side, 8)
    over = 1.0 / (inv[...] * scale)
    band_rows = lax.broadcasted_iota(jnp.int32, (side, size), 0) + begin
    upper = lax.broadcasted_iota(jnp.int32, (side, size), 1) >= band_rows

    @pl.when(good)
    def _():
        band = three(mm, split(x_ref[pl.ds(begin, side), :]), (b_high[...], b_low[...]))
        band_ref[...] = jnp.where(upper, band * over, 0.0)

    @pl.when(jnp.logical_not(good))
    def _():
        band_ref[...] = jnp.where(upper, work[pl.ds(begin, side), :size] * over, 0.0)

    white_ref[...] = scale * three(mm_t, split(feat_ref[...] * inv[...]), split(x_ref[...]))


def shards(
    adapter_input,
    output_gradient,
    projection,
    input_block_index,
    turn_token_length,
    turn_to_example,
):
    layers, count = lax.axis_size("layer"), lax.axis_size("example")
    rank, tokens = adapter_input.shape[1:]
    width = output_gradient.shape[2]
    blocks = projection.shape[1]
    size = blocks * LANES
    peers = count // 2
    pieces = 4
    packed_rows = blocks * (blocks + 1) // 2 * LANES
    owners = 2 * layers * peers
    chunk = -(-packed_rows // (owners * 8)) * 8
    vmem = pl.BlockSpec(memory_space=pltpu.VMEM)
    dma = pltpu.SemaphoreType.DMA
    near, far = max(layers - 1, 1), max(peers - 1, 1)
    gram, features = pl.pallas_call(
        functools.partial(gram_kernel, layers, count, pieces, chunk),
        out_shape=(
            jax.ShapeDtypeStruct((owners * chunk, LANES), F32),
            jax.ShapeDtypeStruct((EX_DEV // layers, size), F32),
        ),
        in_specs=[pl.BlockSpec(memory_space=pltpu.HBM)] * 6,
        out_specs=(vmem, vmem),
        scratch_shapes=[
            pltpu.SMEM(input_block_index.shape[1:], jnp.int32),
            pltpu.VMEM((1, turn_token_length.shape[0]), jnp.int32),
            pltpu.VMEM((1, turn_to_example.shape[0]), jnp.int32),
            pltpu.VMEM((rank, tokens), BF16),
            pltpu.VMEM((tokens, width), BF16),
            pltpu.VMEM(projection.shape[1:], BF16),
            pltpu.VMEM((rank * EX_DEV, tokens), BF16),
            pltpu.VMEM((HALVES, rank * width // LANES, EX_DEV // HALVES, LANES), BF16),
            pltpu.VMEM((EX_DEV, size), F32),
            pltpu.VMEM((near, EX_DEV, size), F32),
            pltpu.VMEM((2, EX_DEV, size), F32),
            pltpu.VMEM((owners * chunk, LANES), F32),
            pltpu.VMEM((far, chunk, LANES), F32),
            dma((5,)), dma((pieces,)),
            dma((near, HALVES)), dma((near, HALVES)), dma((HALVES,)), dma((HALVES,)),
            dma((far,)), dma((far,)), dma((far,)), dma((far,)),
            dma((near, peers)), dma((near, peers)), dma((layers,)), dma((layers,)),
        ],
        compiler_params=pltpu.CompilerParams(
            collective_id=0, has_side_effects=True, vmem_limit_bytes=40 * 1024 * 1024
        ),
    )(*(
        pltpu.with_memory_space_constraint(operand, pltpu.HBM)
        for operand in (
            input_block_index[0],
            turn_token_length.reshape(1, -1),
            turn_to_example.reshape(1, -1),
            adapter_input[0],
            output_gradient[0],
            projection[0],
        )
    ))
    return pl.pallas_call(
        functools.partial(factor_kernel, math.sqrt(EX_DEV * count), blocks),
        out_shape=(
            jax.ShapeDtypeStruct((size // count, size), F32),
            jax.ShapeDtypeStruct((EX_DEV // layers, size), F32),
        ),
        in_specs=[vmem, vmem],
        out_specs=(vmem, vmem),
        scratch_shapes=[
            pltpu.VMEM((size, size), F32),
            pltpu.VMEM((size, size), BF16),
            pltpu.VMEM((size, size), BF16),
            pltpu.VMEM((size, size), F32),
            pltpu.VMEM((size, size), BF16),
            pltpu.VMEM((1, size), F32),
            pltpu.VMEM((size, 2 * size), F32),
        ],
        compiler_params=pltpu.CompilerParams(vmem_limit_bytes=40 * 1024 * 1024),
    )(gram, features)


def solution(mesh):
    in_specs = (
        P("layer", None, "example"),
        P("layer", "example", None),
        P("layer", None, None, None),
        P("layer", None, None),
        P("example"),
        P("example"),
    )
    out_specs = (P("example", None), P(("example", "layer"), None))
    return jax.shard_map(shards, mesh=mesh, in_specs=in_specs, out_specs=out_specs, check_vma=False)
```
